256 devices in a mesh: dp: 4 (over y_hi, core), fsdp: 64 (over z, y_lo, x).
Axes of the slice: x: 4, y: 4 (y_hi: 2, y_lo: 2; y = y_hi * 2 + y_lo), z: 8, core: 2. Of those that a mesh axis runs over, the one named last changes fastest.
Arguments:
- inputs: bfloat16 [256, 512, 768], P(('dp', 'fsdp')), may hold values from -6 to 6
- segment_ids: int32 [256, 512], P(('dp', 'fsdp')), may hold values from 0 to 3, never falling along the last dimension, each value on 1 to 256 neighbouring positions
- cotangent: bfloat16 [256, 512, 768], P(('dp', 'fsdp')), may hold values from -24 to 24
- qkv_weight: bfloat16 [768, 2304], P('fsdp'), may hold values from -0.21875 to 0.21875
- query_bias: bfloat16 [768], P('fsdp'), may hold values from -3 to 3
- value_bias: bfloat16 [768], P('fsdp'), may hold values from -0.59765625 to 0.59765625
- out_weight: bfloat16 [768, 768], P('fsdp'), may hold values from -2.5 to 2.5
- out_bias: bfloat16 [768], P('fsdp'), may hold values from -1.1953125 to 1.1953125
- attn_gain: bfloat16 [768], P('fsdp'), may hold values from 0.25 to 1.75
- attn_shift: bfloat16 [768], P('fsdp'), may hold values from -1.1953125 to 1.1953125
- up_weight: bfloat16 [768, 3072], P('fsdp'), may hold values from -0.21875 to 0.21875
- up_bias: bfloat16 [3072], P('fsdp'), may hold values from -1.796875 to 1.796875
- down_weight: bfloat16 [3072, 768], P('fsdp'), may hold values from -0.15625 to 0.15625
- down_bias: bfloat16 [768], P('fsdp'), may hold values from -1.1953125 to 1.1953125
- ffn_gain: bfloat16 [768], P('fsdp'), may hold values from 0.25 to 1.75
- ffn_shift: bfloat16 [768], P('fsdp'), may hold values from -1.1953125 to 1.1953125
Outputs:
- outputs: bfloat16 [256, 512, 768], P(('dp', 'fsdp'))
- input_grad: bfloat16 [256, 512, 768], P(('dp', 'fsdp'))
- qkv_weight_grad: float32 [768, 2304], P('fsdp')
- query_bias_grad: float32 [768], P('fsdp')
- value_bias_grad: float32 [768], P('fsdp')
- out_weight_grad: float32 [768, 768], P('fsdp')
- out_bias_grad: float32 [768], P('fsdp')
- attn_gain_grad: float32 [768], P('fsdp')
- attn_shift_grad: float32 [768], P('fsdp')
- up_weight_grad: float32 [768, 3072], P('fsdp')
- up_bias_grad: float32 [3072], P('fsdp')
- down_weight_grad: float32 [3072, 768], P('fsdp')
- down_bias_grad: float32 [768], P('fsdp')
- ffn_gain_grad: float32 [768], P('fsdp')
- ffn_shift_grad: float32 [768], P('fsdp')
The draws below stay inside these ranges and needn't reach their ends.
Inputs may be any that keep to these rules, and one draw needn't show every extreme that they name: `segment_ids`: on every page the segment numbers never fall; each segment holds 1 to half of 512 tokens, one exactly that many.
All inputs are finite; a program needn't handle non-finite values.
Results may differ from the reference program's by a relative error of at most 0.022.
Values may be sent and summed in bfloat16 or wider, within the bound.
A program may use at most 128 MiB of HBM per device.

```python
import math
import jax
import jax.numpy as jnp
import numpy as np
from jax import lax

D = 768
HEADS = 12
HD = 64
FF = 3072
SEQ_LEN = 512
SEGMENTS = 4
SEQS = 256


def with_spikes(values, key, source, target, blocks, factor):
    def block_of(position):
        return (jnp.arange(values.shape[position]) // (values.shape[position] // blocks)).reshape((-1,) + (1,) * (values.ndim - 1 - position))

    first = jax.random.permutation(key, blocks)[block_of(target)]
    second = (block_of(target) + blocks // 2) % blocks
    return jnp.where((block_of(source) == first) | (block_of(source) == second), factor * values, values)


def block_scale(stream_key, extent, pieces, least, high):
    level = 1.0
    for dim, shards_of in pieces:
        draws = jax.random.uniform(jax.random.fold_in(jax.random.fold_in(stream_key, 6), dim), (shards_of,), jnp.float32, least / len(pieces), high / len(pieces))
        level = level * jnp.repeat(jnp.exp(draws), extent[dim] // shards_of).reshape((-1,) + (1,) * (len(extent) - 1 - dim))
    return level


def length_profile(number_of, total, limit, skew):
    weights = [(1 << 20) // math.isqrt(rank ** skew) + 1 for rank in range(2, number_of + 1)]
    surplus, given = total - limit - (number_of - 1), [1] * (number_of - 1)
    while surplus > 0:
        movable = [i for i in range(number_of - 1) if given[i] < limit]
        whole, budget = sum([weights[i] for i in movable]), surplus
        for i in movable:
            more = min(limit - given[i], max(1, budget * weights[i] // whole), surplus)
            given[i] = given[i] + more
            surplus = surplus - more
    return np.array([limit] + given)


def ragged(stream_key, number_of, total, bound, skew):
    if number_of == 2:
        one = jax.random.randint(stream_key, (), max(1, total - bound), min(bound, total - 1) + 1)
        return jnp.stack([one, total - one])
    lengths = jnp.asarray(length_profile(number_of, total, bound, skew), jnp.int32)
    pairs = (number_of - 1) // 2
    source_of, sink = lengths[1:1 + 2 * pairs:2], lengths[2:2 + 2 * pairs:2]
    room = jnp.minimum(source_of - 1, bound - sink)
    shifted = jax.random.randint(jax.random.fold_in(stream_key, 1), (pairs,), 0, 1 << 20) % (room + 1)
    lengths = lengths.at[1:1 + 2 * pairs:2].set(source_of - shifted).at[2:2 + 2 * pairs:2].set(sink + shifted)
    return lengths[jax.random.permutation(jax.random.fold_in(stream_key, 2), number_of)]


def noise(own_key, dims, scale, reach, split=(), kind=jnp.bfloat16):
    drawn = scale * jax.random.normal(own_key, dims, jnp.float32)
    if split:
        drawn = drawn * block_scale(own_key, dims, split, -0.22, 0.18)
    return jnp.clip(drawn, -reach, reach).astype(kind)


def heavy_noise(rng, dims, width, limit, shards, heavy, held_as=jnp.bfloat16):
    entries = width * jax.random.normal(rng, dims, jnp.float32)
    if shards:
        entries = entries * block_scale(rng, dims, shards, -0.22, 0.18)
    return jnp.clip(with_spikes(entries, jax.random.fold_in(rng, 3), *heavy), -limit, limit).astype(held_as)


def setup_inputs(seed: int = 0) -> dict:
    keys = jax.random.split(jax.random.key(seed), 17)
    return {
        "inputs": noise(keys[0], (SEQS, SEQ_LEN, D), 1.0, 6.0, ((0, 256),)),
        "segment_ids": jax.vmap(lambda own: jnp.searchsorted(jnp.cumsum(ragged(own, SEGMENTS, SEQ_LEN, SEQ_LEN // 2, 1)), jnp.arange(SEQ_LEN), side="right"))(jax.random.split(keys[1], SEQS)).reshape((SEQS, SEQ_LEN)).astype(jnp.int32),
        "cotangent": heavy_noise(keys[2], (SEQS, SEQ_LEN, D), 1.0, 24.0, ((0, 256),), (0, 2, 256, 6.0)),
        "qkv_weight": noise(keys[3], (D, 3 * D), D ** -0.5, 0.21875, ((0, 64),)),
        "query_bias": noise(keys[4], (D,), 0.5, 3.0, ((0, 64),)),
        "value_bias": noise(keys[5], (D,), 0.1, 0.59765625, ((0, 64),)),
        "out_weight": noise(keys[6], (D, D), (max(D // 128, 1)) ** -0.5, 2.5, ((0, 64),)),
        "out_bias": noise(keys[7], (D,), 0.2, 1.1953125, ((0, 64),)),
        "attn_gain": jnp.clip(1.0 + 0.15 * jax.random.normal(keys[8], (D,), jnp.float32), 0.25, 1.75).astype(jnp.bfloat16),
        "attn_shift": noise(keys[9], (D,), 0.2, 1.1953125, ((0, 64),)),
        "up_weight": noise(keys[10], (D, FF), D ** -0.5, 0.21875, ((0, 64),)),
        "up_bias": noise(keys[11], (FF,), 0.3, 1.796875, ((0, 64),)),
        "down_weight": noise(keys[12], (FF, D), (FF // 2) ** -0.5, 0.15625, ((0, 64),)),
        "down_bias": noise(keys[13], (D,), 0.2, 1.1953125, ((0, 64),)),
        "ffn_gain": jnp.clip(1.0 + 0.15 * jax.random.normal(keys[14], (D,), jnp.float32), 0.25, 1.75).astype(jnp.bfloat16),
        "ffn_shift": noise(keys[15], (D,), 0.2, 1.1953125, ((0, 64),)),
    }


@jax.custom_vjp
def low(v):
    return lax.optimization_barrier(v.astype(jnp.bfloat16)).astype(jnp.float32)

@jax.custom_vjp
def low_back(v):
    return v

def low_keep(v):
    return (low(v), None)

def low_pass(kept, grad):
    return (grad,)

def back_keep(v):
    return (v, None)

def back_low(kept, grad):
    return (low(grad),)
low.defvjp(low_keep, low_pass)
low_back.defvjp(back_keep, back_low)

def scaled_rows(values, gain):
    centre = lax.optimization_barrier(jnp.mean(values, axis=-1, keepdims=True))
    centred = values - centre
    spread = lax.optimization_barrier(jnp.mean(centred * centred, axis=-1, keepdims=True))
    return centred * lax.rsqrt(spread + 1e-12) * gain

def gelu_exact(values):
    return 0.5 * values * (1.0 + lax.erf(values * 0.7071067811865476))

def project(left, right):
    return jnp.einsum('gtd,de->gte', left, right, precision=lax.Precision.HIGHEST)

def layer_block(params, block):
    qkv_weight, query_bias, value_bias, out_weight, out_bias, attn_gain, attn_shift, up_weight, up_bias, down_weight, down_bias, ffn_gain, ffn_shift = params
    hidden_in, segment_ids = block
    group_count = hidden_in.shape[0]
    head_shape = (group_count, SEQ_LEN, HEADS, HD)
    projected = project(hidden_in, qkv_weight)
    query_heads = low_back(low(projected[..., :D] + query_bias)).reshape(head_shape)
    key_heads = low_back(low(projected[..., D:2 * D])).reshape(head_shape)
    value_heads = low_back(low(projected[..., 2 * D:] + value_bias)).reshape(head_shape)
    score_scale = 1.0 / math.sqrt(HD)
    scores = jnp.einsum('gqhd,gkhd->ghqk', query_heads, key_heads, precision=lax.Precision.HIGHEST)
    scores = low_back(scores * score_scale)
    same_segment = segment_ids[:, None, :, None] == segment_ids[:, None, None, :]
    scores = jnp.where(same_segment, scores, -1e+30)
    row_peak = lax.optimization_barrier(jnp.max(scores, axis=-1, keepdims=True))
    exp_terms = jnp.exp(scores - row_peak)
    softmax_weights = exp_terms / lax.optimization_barrier(jnp.sum(exp_terms, axis=-1, keepdims=True))
    context = jnp.einsum('ghqk,gkhd->gqhd', low(softmax_weights), value_heads, precision=lax.Precision.HIGHEST)
    context = low_back(low(context)).reshape(group_count, SEQ_LEN, D)
    attended = low_back(project(context, out_weight) + out_bias)
    first_norm = low(scaled_rows(hidden_in + attended, attn_gain) + attn_shift)
    ffn_inner = low_back(project(first_norm, up_weight) + up_bias)
    active = low(gelu_exact(ffn_inner))
    branch = low_back(project(active, down_weight) + down_bias)
    return scaled_rows(first_norm + branch, ffn_gain) + ffn_shift

def reference(inputs, segment_ids, cotangent, qkv_weight, query_bias, value_bias, out_weight, out_bias, attn_gain, attn_shift, up_weight, up_bias, down_weight, down_bias, ffn_gain, ffn_shift):
    params = tuple((entry.astype(jnp.float32) for entry in (qkv_weight, query_bias, value_bias, out_weight, out_bias, attn_gain, attn_shift, up_weight, up_bias, down_weight, down_bias, ffn_gain, ffn_shift)))
    hidden = inputs.astype(jnp.float32)
    per_block = math.gcd(SEQS, 8)
    block_count = SEQS // per_block
    segment_blocks = segment_ids.reshape(block_count, per_block, SEQ_LEN)

    def forward(hidden_all, params_all):

        def apply(block):
            return layer_block(params_all, block)
        stacked = lax.map(jax.checkpoint(apply), (hidden_all.reshape(block_count, per_block, SEQ_LEN, D), segment_blocks))
        return stacked.reshape(SEQS, SEQ_LEN, D)
    outputs, pullback = jax.vjp(forward, hidden, params)
    input_grad, grads = pullback(cotangent.astype(jnp.float32))
    return (outputs.astype(jnp.bfloat16), input_grad.astype(jnp.bfloat16), grads[0], grads[1], grads[2], grads[3], grads[4], grads[5], grads[6], grads[7], grads[8], grads[9], grads[10], grads[11], grads[12])
```

```python
import functools
import types

import jax
import jax.numpy as jnp
from jax import lax
from jax.experimental import pallas as pl
from jax.experimental.pallas import tpu as pltpu
from jax.sharding import PartitionSpec as P

T = 512
D = 768
FF = 3072
BF = jnp.bfloat16
F32 = jnp.float32
MESH = pl.DeviceIdType.MESH
BLOCK = (2, 4, 2, 4, 48, 256)

SCRATCH = (
    ("G", pltpu.VMEM((9,) + BLOCK, BF)),
    ("GV", pltpu.VMEM((2, 4, 2, 4, 16, 128), BF)),
    ("gr", pltpu.VMEM((4,) + BLOCK, BF)),
    ("rd", pltpu.VMEM((6, 4, 2, 4, 48, 256), BF)),
    ("r1", pltpu.VMEM((6, 3, 4, 2, 48, 256), BF)),
    ("r2", pltpu.VMEM((6, 7, 2, 48, 256), BF)),
    ("r3", pltpu.VMEM((6, 4, 48, 256), BF)),
    ("fin", pltpu.VMEM((9, 48, 256), F32)),
    ("qkv", pltpu.VMEM((3, 3, T, 256), BF)),
    ("p", pltpu.VMEM((12, T, T), BF)),
    ("mask", pltpu.VMEM((T, T), BF)),
    ("ctx", pltpu.VMEM((T, D), BF)),
    ("n1", pltpu.VMEM((T, D), F32)),
    ("rs1", pltpu.VMEM((T, 128), F32)),
    ("fn", pltpu.VMEM((T, D), BF)),
    ("act", pltpu.VMEM((4, 3 * T, 256), BF)),
    ("slope", pltpu.VMEM((4, T, D), BF)),
    ("acc", pltpu.VMEM((T, D), F32)),
    ("gb", pltpu.VMEM((T, D), BF)),
    ("tr", pltpu.VMEM((D, T), BF)),
    ("perm", pltpu.VMEM((192, 192), BF)),
    ("vec", pltpu.VMEM((16, D), F32)),
    ("ub", pltpu.VMEM((8, FF), F32)),
    ("vg", pltpu.VMEM((16, D), F32)),
    ("va", pltpu.VMEM((14, 8, D), F32)),
    ("vo", pltpu.VMEM((3, 8, D), F32)),
    ("small", pltpu.VMEM((16, 128), F32)),
    ("own", pltpu.VMEM((48, 256), F32)),
)
SEMS = (
    ("zs", (10, 7)), ("zr", (10, 4)), ("xs", (10, 3)), ("xr", (10, 3)),
    ("ys", (10, 2)), ("yr", (10, 2)), ("ds", (10,)), ("dr", (10,)),
    ("rds", (9,)), ("rdr", (9,)), ("p1s", (9, 3)), ("p1r", (9, 3)),
    ("p2s", (9, 4)), ("p2r", (9, 7)), ("p3s", (9, 4)), ("p3r", (9, 4)),
    ("fs", (9,)), ("fr", (9,)), ("vs", (15,)), ("vr", (15,)),
)
INS = (
    "x", "seg", "ct", "wqkv", "qb", "vb", "wout", "ob", "ag", "ash",
    "wup", "ub_in", "wdown", "db", "fg", "fsh",
)
OUTS = ("o_out", "o_ig", "o_qkv", "o_wout", "o_up", "o_down", "o_vec")


def dot(a, b):
    return lax.dot_general(a, b, (((1,), (0,)), ((), ())), preferred_element_type=F32)


def dot_nt(a, b):
    return lax.dot_general(a, b, (((1,), (1,)), ((), ())), preferred_element_type=F32)


def dot_tn(a, b):
    return lax.dot_general(a, b, (((0,), (0,)), ((), ())), preferred_element_type=F32)


def device(x, y, z, c):
    return ((y // 2) * 2 + c, z * 8 + lax.rem(y, 2) * 4 + x)


def kernel(*refs):
    names = INS + OUTS + tuple(n for n, _ in SCRATCH) + tuple(n for n, _ in SEMS) + ("ready",)
    s = types.SimpleNamespace(**dict(zip(names, refs, strict=True)))
    dp, fs = lax.axis_index("dp"), lax.axis_index("fsdp")
    C = lax.rem(dp, 2)
    YH = dp // 2
    Z = fs // 8
    YL = lax.rem(fs // 4, 2)
    X = lax.rem(fs, 4)
    Y = YH * 2 + YL
    ZT = Z // 4
    ZL = lax.rem(Z, 4)

    def copy(src, dst, send, recv, where):
        return pltpu.make_async_remote_copy(
            src_ref=src, dst_ref=dst, send_sem=send, recv_sem=recv, device_id=where, device_id_type=MESH
        )

    sibling = device(X, Y, Z, 1 - C)
    partners = (
        [sibling]
        + [device(lax.rem(X + d, 4), Y, Z, C) for d in (1, 2, 3)]
        + [device(X, lax.rem(Y + d, 4), Z, C) for d in (1, 2, 3)]
        + [device(X, Y, lax.rem(Z + d, 8), C) for d in range(1, 8)]
        + [device(lax.rem(X + d, 4), lax.rem(Y + 2, 4), Z, C) for d in (1, 2, 3)]
    )

    def greet(sem):
        for where in partners:
            pl.semaphore_signal(sem, inc=1, device_id=where, device_id_type=MESH)

    def gref(k):
        return s.GV if isinstance(k, int) and k == 9 else s.G.at[k]

    def z_copy(k, d):
        here = gref(k).at[ZT, ZL, YL, X]
        return copy(here, here, s.zs.at[k, d - 1], s.zr.at[k, ZL], device(X, Y, lax.rem(Z + d, 8), C))

    def z_recv(k, zl):
        here = gref(k).at[C, zl, YL, X]
        return copy(here, here, s.zs.at[k, 0], s.zr.at[k, zl], sibling)

    def x_copy(k, d):
        here = gref(k).at[C, :, YL, X]
        return copy(here, here, s.xs.at[k, d - 1], s.xr.at[k, d - 1], device(lax.rem(X + d, 4), Y, Z, C))

    def y_copy(k, i):
        here = gref(k).at[C, :, YL, pl.ds(2 * i, 2)]
        return copy(here, here, s.ys.at[k, i], s.yr.at[k, i], device(X, lax.rem(Y + 1 + 2 * i, 4), Z, C))

    def d_copy(k):
        here = gref(k).at[C]
        return copy(here, here, s.ds.at[k], s.dr.at[k], sibling)

    def ag_z(k):
        @pl.when(C == ZT)
        def _():
            for d in (4, 3, 5, 2, 6, 1, 7):
                z_copy(k, d).start()

    def ag_x(k):
        for zl in range(4):
            @pl.when(jnp.logical_or(C != ZT, zl != ZL))
            def _():
                z_recv(k, zl).wait_recv()
        for d in (2, 1, 3):
            x_copy(k, d).start()

    def ag_y(k):
        for d in (1, 2, 3):
            x_copy(k, d).wait_recv()
        for i in (0, 1):
            y_copy(k, i).start()

    def ag_d(k):
        for i in (0, 1):
            y_copy(k, i).wait_recv()
        d_copy(k).start()

    def ag_done(k):
        d_copy(k).wait()
        @pl.when(C == ZT)
        def _():
            for d in range(1, 8):
                z_copy(k, d).wait_send()
        for d in (1, 2, 3):
            x_copy(k, d).wait_send()
        for i in (0, 1):
            y_copy(k, i).wait_send()

    def ag_tick(t):
        for lag, step in ((2, ag_d), (1, ag_y), (0, ag_x)):
            i = t - lag
            if i == 0:
                step(9)
            if 0 <= i <= 8:
                step(i)

    def own_block(k, parts):
        for m, part in enumerate(parts):
            s.own[12 * m : 12 * m + 12, :] = part.astype(F32)
        s.G[k, ZT, ZL, YL, X] = s.own[...].astype(BF)

    for g in range(3):
        lo = 256 * g
        own_block(g, [s.wqkv[:, m * D + lo : m * D + lo + 256] for m in range(3)] + [s.wout[:, lo : lo + 256]])
    for g in range(3):
        lo = 256 * g
        own_block(3 + g, [s.wup[:, m * D + lo : m * D + lo + 256] for m in range(4)])
        s.G[6 + g, ZT, ZL, YL, X] = s.wdown[:, lo : lo + 256]
    s.small[...] = jnp.zeros((16, 128), F32)
    for i, v in enumerate((s.qb, s.vb, s.ob, s.ag, s.ash, s.db, s.fg, s.fsh)):
        s.small[i : i + 1, 0:12] = v[...].astype(F32)
    s.small[8:9, 0:48] = s.ub_in[...].astype(F32)
    s.GV[ZT, ZL, YL, X] = s.small[...].astype(BF)

    barrier = pltpu.get_barrier_semaphore()
    greet(barrier)
    pl.semaphore_wait(barrier, len(partners))

    ag_z(9)
    for k in range(9):
        ag_z(k)

    row = lax.broadcasted_iota(jnp.int32, (192, 192), 0)
    col = lax.broadcasted_iota(jnp.int32, (192, 192), 1)
    swapped = lax.rem(row // 12, 4) * 48 + (row // 48) * 12 + lax.rem(row, 12)
    s.perm[...] = (col == swapped).astype(F32).astype(BF)
    segf = jnp.broadcast_to(s.seg[...].astype(F32), (128, T))
    seg_col = jnp.transpose(segf)[:, 0:1]
    s.mask[...] = jnp.where(seg_col == segf[0:1, :], 0.0, -1e30).astype(BF)
    s.vg[...] = jnp.zeros((16, D), F32)

    def reorder(src, dst):
        @pl.loop(0, 16)
        def _(i):
            a, b, c = i // 8, lax.rem(i // 2, 4), lax.rem(i, 2)
            v = src[a, b, c].reshape(192, 256)
            w = dot(s.perm[...], v).astype(BF)
            dst[a, b, c] = w.reshape(4, 48, 256)

    def weight(k, m):
        return s.G[k, :, :, :, m].reshape(D, 256)

    def weight_row(base, m):
        return jnp.concatenate([weight(base + g, m) for g in range(3)], axis=1)

    def down_rows(m):
        parts = [s.G[6 + g, m // 2, pl.ds(2 * (m % 2), 2)].reshape(D, 256) for g in range(3)]
        return jnp.concatenate(parts, axis=1)

    def active(m):
        return jnp.concatenate([s.act[m, T * g : T * g + T] for g in range(3)], axis=1)

    ag_tick(0)
    ag_tick(1)
    ag_tick(2)
    ag_done(9)

    pick_r = lax.broadcasted_iota(jnp.int32, (128, D), 0)
    pick_c = lax.broadcasted_iota(jnp.int32, (128, D), 1)
    s.vec[...] = jnp.zeros((16, D), F32)
    s.ub[...] = jnp.zeros((8, FF), F32)

    @pl.loop(0, 8)
    def _(i):
        gv = s.GV[i // 4, lax.rem(i, 4)].reshape(128, 128)
        wide = dot(gv, (lax.rem(pick_c, 12) == pick_r).astype(F32).astype(BF))
        owner = lax.broadcasted_iota(jnp.int32, (128, D), 0) // 16 + 8 * i
        lane = lax.broadcasted_iota(jnp.int32, (128, D), 1) // 12
        s.vec[...] += jnp.sum(jnp.where(owner == lane, wide, 0.0).reshape(8, 16, D), axis=0)
        sel_r = lax.broadcasted_iota(jnp.int32, (8, 128), 0)
        sel_c = lax.broadcasted_iota(jnp.int32, (8, 128), 1)
        rows8 = dot((sel_c == 16 * sel_r + 8).astype(F32).astype(BF), gv).astype(BF)
        for m in range(4):
            up_c = pick_c + m * D
            wide_up = dot(rows8, (lax.rem(up_c, 48) == pick_r).astype(F32).astype(BF))
            own_r = lax.broadcasted_iota(jnp.int32, (8, D), 0) + 8 * i
            own_c = (lax.broadcasted_iota(jnp.int32, (8, D), 1) + m * D) // 48
            s.ub[:, m * D : m * D + D] += jnp.where(own_r == own_c, wide_up, 0.0)

    s.ub[0:1, :] = jnp.sum(s.ub[...], axis=0, keepdims=True)

    head_lane = lax.broadcasted_iota(jnp.int32, (1, 128), 1) // 64

    def head_only(v, h):
        return jnp.where(head_lane == h, v, jnp.zeros_like(v))

    for g in range(3):
        ag_done(g)
        reorder(s.G.at[g], s.G.at[g])
        ag_tick(3 + 2 * g)
        xv = s.x[...]
        for m in range(3):
            v = dot(xv, weight(g, m))
            if m != 1:
                i = 0 if m == 0 else 1
                v = v + s.vec[i : i + 1, 256 * g : 256 * g + 256]
            s.qkv[m, g] = v.astype(BF)
        ag_tick(4 + 2 * g)

        @pl.loop(0, 2)
        def _(j):
            lanes = pl.ds(pl.multiple_of(j * 128, 128), 128)
            q = s.qkv[0, g, :, lanes] * 0.125
            k = s.qkv[1, g, :, lanes]
            v = s.qkv[2, g, :, lanes]
            out = jnp.zeros((T, 128), F32)
            for h in range(2):
                sc = dot_nt(head_only(q, h), k) + s.mask[...].astype(F32)
                e = jnp.exp(sc - jnp.max(sc, axis=1, keepdims=True))
                w = (e * (1.0 / jnp.sum(e, axis=1, keepdims=True))).astype(BF)
                s.p[4 * g + 2 * j + h] = w
                out = out + dot(w, head_only(v, h))
            s.ctx[:, pl.ds(pl.multiple_of(g * 256 + j * 128, 128), 128)] = out.astype(BF)

    ag_tick(9)
    cv = s.ctx[...]
    for g in range(3):
        s.acc[:, 256 * g : 256 * g + 256] = dot(cv, weight(g, 3))
    ag_tick(10)

    @pl.loop(0, 16)
    def _(i):
        rows = pl.ds(pl.multiple_of(i * 32, 32), 32)
        v = s.acc[rows, :] + s.vec[2:3, :] + s.x[rows, :].astype(F32)
        v = v - jnp.mean(v, axis=1, keepdims=True)
        r = lax.rsqrt(jnp.mean(v * v, axis=1, keepdims=True) + 1e-12)
        n = v * r
        s.n1[rows, :] = n
        s.rs1[rows, :] = jnp.broadcast_to(r, (32, 128))
        s.fn[rows, :] = (n * s.vec[3:4, :] + s.vec[4:5, :]).astype(BF)

    fv = s.fn[...]
    for g in range(3):
        ag_done(3 + g)
        reorder(s.G.at[3 + g], s.G.at[3 + g])
        for m in range(4):
            lo = 256 * g
            u = dot(fv, weight(3 + g, m)) + s.ub[0:1, m * D + lo : m * D + lo + 256]
            half = 0.5 * (1.0 + lax.erf(u * 0.7071067811865476))
            s.act[m, T * g : T * g + T] = (u * half).astype(BF)
            s.slope[m, :, lo : lo + 256] = (half + u * jnp.exp(-0.5 * u * u) * 0.3989422804014327).astype(BF)
    for g in range(3):
        ag_done(6 + g)
        lo = 256 * g
        total = jnp.zeros((T, 256), F32)
        for m in range(4):
            total = total + dot(active(m), s.G[6 + g, m // 2, 2 * (m % 2) : 2 * (m % 2) + 2].reshape(D, 256))
        s.acc[:, lo : lo + 256] = total

    @pl.loop(0, 16)
    def _(i):
        rows = pl.ds(pl.multiple_of(i * 32, 32), 32)
        v = s.acc[rows, :] + s.vec[5:6, :] + s.fn[rows, :].astype(F32)
        v = v - jnp.mean(v, axis=1, keepdims=True)
        r = lax.rsqrt(jnp.mean(v * v, axis=1, keepdims=True) + 1e-12)
        n = v * r
        gain = s.vec[6:7, :]
        s.o_out[rows, :] = (n * gain + s.vec[7:8, :]).astype(BF)
        u = s.ct[rows, :].astype(F32)
        ug = u * gain
        un = u * n
        grad = r * (ug - jnp.mean(ug, axis=1, keepdims=True) - n * jnp.mean(ug * n, axis=1, keepdims=True))
        low = grad.astype(BF)
        s.acc[rows, :] = grad
        s.gb[rows, :] = low
        s.vg[5:6, :] += jnp.sum(low.astype(F32), axis=0, keepdims=True)
        s.vg[6:7, :] += jnp.sum(un, axis=0, keepdims=True)
        s.vg[7:8, :] += jnp.sum(u, axis=0, keepdims=True)

    def rd_copy(j):
        return copy(
            s.gr.at[j % 4, 1 - C], s.rd.at[j % 6], s.rds.at[j], s.rdr.at[j], sibling
        )

    def p1_copy(j, d, c):
        if c == 0:
            xx = lax.rem(X + d, 4)
            src, where = s.gr.at[j % 4, 0, :, :, xx], device(xx, Y, Z, 0)
        else:
            yy = lax.rem(Y + d, 4)
            src = s.gr.at[j % 4, 1, :, lax.rem(yy, 2), pl.ds(2 * (yy // 2), 2)]
            where = device(X, yy, Z, 1)
        return copy(src, s.r1.at[j % 6, d - 1], s.p1s.at[j, d - 1], s.p1r.at[j, d - 1], where)

    def p2_copy(j, zl):
        zz = C * 4 + zl
        slot = lax.rem(Z - zz + 8, 8) - 1
        return copy(
            s.r1.at[j % 6, 0, zl], s.r2.at[j % 6, slot], s.p2s.at[j, zl], s.p2r.at[j, slot],
            device(X, Y, zz, C),
        )

    def p2_recv(j, slot):
        return copy(
            s.r1.at[j % 6, 0, 0], s.r2.at[j % 6, slot], s.p2s.at[j, 0], s.p2r.at[j, slot], sibling
        )

    def p3_copy0(j, d):
        yy = lax.rem(Y + d, 4)
        return copy(
            s.r2.at[j % 6, 0, lax.rem(yy, 2)], s.r3.at[j % 6, Y], s.p3s.at[j, d], s.p3r.at[j, Y],
            device(X, yy, Z, 0),
        )

    def p3_copy1(j, i, other):
        xx = 2 * YH + i
        yy = lax.rem(Y + 2 * other, 4)
        return copy(
            s.r2.at[j % 6, 0, i], s.r3.at[j % 6, X], s.p3s.at[j, 2 * i + other], s.p3r.at[j, X],
            device(xx, yy, Z, 1),
        )

    def p3_recv(j, slot):
        return copy(
            s.r2.at[j % 6, 0, 0], s.r3.at[j % 6, slot], s.p3s.at[j, 0], s.p3r.at[j, slot], sibling
        )

    def f_copy(j):
        here = s.fin.at[j]
        return copy(here, here, s.fs.at[j], s.fr.at[j], sibling)

    def rs_d(j):
        rd_copy(j).start()

    def rs_p1(j):
        rd_copy(j).wait()

        @pl.loop(0, 8)
        def _(i):
            a, b = i // 2, lax.rem(i, 2)
            v = s.gr[j % 4, C, a, b].astype(F32) + s.rd[j % 6, a, b].astype(F32)
            s.gr[j % 4, C, a, b] = v.astype(BF)

        for c in (0, 1):
            @pl.when(C == c)
            def _():
                for d in (2, 1, 3):
                    p1_copy(j, d, c).start()

    def rs_p2(j):
        for c in (0, 1):
            @pl.when(C == c)
            def _():
                for d in (1, 2, 3):
                    p1_copy(j, d, c).wait()

        @pl.loop(0, 8)
        def _(i):
            a, b = i // 2, lax.rem(i, 2)
            mine = s.gr[j % 4, C, a, jnp.where(C == 0, b, YL), jnp.where(C == 0, X, 2 * YH + b)]
            v = mine.astype(F32)
            for d in range(3):
                v = v + s.r1[j % 6, d, a, b].astype(F32)
            s.r1[j % 6, 0, a, b] = v.astype(BF)

        for zl in range(4):
            @pl.when(C * 4 + zl != Z)
            def _():
                p2_copy(j, zl).start()

    def rs_p3(j):
        @pl.when(C == ZT)
        def _():
            for slot in range(7):
                p2_recv(j, slot).wait_recv()
            for b in range(2):
                v = s.r1[j % 6, 0, ZL, b].astype(F32)
                for slot in range(7):
                    v = v + s.r2[j % 6, slot, b].astype(F32)
                s.r2[j % 6, 0, b] = v.astype(BF)

        @pl.when(jnp.logical_and(C == 0, ZT == 0))
        def _():
            for d in (1, 2, 3):
                p3_copy0(j, d).start()

        @pl.when(jnp.logical_and(C == 1, ZT == 1))
        def _():
            for i in range(2):
                p3_copy1(j, i, 1).start()

                @pl.when(X != 2 * YH + i)
                def _():
                    p3_copy1(j, i, 0).start()

    def rs_f(j):
        own_slot = jnp.where(C == 0, Y, X)
        has_own = jnp.logical_or(C == 0, YH == X // 2)

        @pl.when(C == ZT)
        def _():
            @pl.when(has_own)
            def _():
                s.r3[j % 6, own_slot] = s.r2[j % 6, 0, jnp.where(C == 0, YL, lax.rem(X, 2))]
            for slot in range(4):
                @pl.when(jnp.logical_not(jnp.logical_and(has_own, own_slot == slot)))
                def _():
                    p3_recv(j, slot).wait_recv()
            v = s.r3[j % 6, 0].astype(F32)
            for slot in range(1, 4):
                v = v + s.r3[j % 6, slot].astype(F32)
            s.fin[j] = v
            f_copy(j).start()

    def rs_done(j):
        for zl in range(4):
            @pl.when(C * 4 + zl != Z)
            def _():
                p2_copy(j, zl).wait_send()

        @pl.when(jnp.logical_and(C == 0, ZT == 0))
        def _():
            for d in (1, 2, 3):
                p3_copy0(j, d).wait_send()

        @pl.when(jnp.logical_and(C == 1, ZT == 1))
        def _():
            for i in range(2):
                p3_copy1(j, i, 1).wait_send()

                @pl.when(X != 2 * YH + i)
                def _():
                    p3_copy1(j, i, 0).wait_send()

        @pl.when(C == ZT)
        def _():
            f_copy(j).wait_send()

        @pl.when(C != ZT)
        def _():
            f_copy(j).wait_recv()

    def rs_tick(t):
        for lag, step in ((4, rs_done), (3, rs_f), (2, rs_p3), (1, rs_p2), (0, rs_p1)):
            if 0 <= t - lag <= 5:
                step(t - lag)

    gbv = s.gb[...]
    for m in range(4):
        s.tr[...] = jnp.transpose(active(m))
        for g in range(3):
            v = dot(s.tr[...], gbv[:, 256 * g : 256 * g + 256])
            s.gr[g, m // 2, 2 * (m % 2) : 2 * (m % 2) + 2] = v.astype(BF).reshape(2, 2, 4, 48, 256)
    for g in range(3):
        rs_d(g)
    for m in range(4):
        low = (dot_nt(gbv, down_rows(m)) * s.slope[m].astype(F32)).astype(BF)
        s.slope[m] = low
        s.vg[8 + m : 9 + m, :] = jnp.sum(low.astype(F32), axis=0, keepdims=True)
    rs_tick(0)
    @pl.loop(0, 4)
    def _(m):
        s.acc[...] += dot_nt(s.slope[m], weight_row(3, m))

    rs_tick(1)
    s.tr[...] = jnp.transpose(s.fn[...])

    def up_chunk(g):
        for m in range(4):
            v = dot(s.tr[...], s.slope[m, :, 256 * g : 256 * g + 256])
            s.act[m, 0:D] = v.astype(BF)

    def put_chunk(slot):
        @pl.loop(0, 16)
        def _(i):
            a, b, c = i // 8, lax.rem(i // 2, 4), lax.rem(i, 2)
            v = s.act[:, pl.ds(pl.multiple_of(48 * i, 16), 48)].reshape(192, 256)
            s.gr[slot, a, b, c] = dot(s.perm[...], v).astype(BF).reshape(4, 48, 256)

    @pl.loop(0, 16)
    def _(i):
        rows = pl.ds(pl.multiple_of(i * 32, 32), 32)
        u = s.acc[rows, :]
        n = s.n1[rows, :]
        r = s.rs1[rows, 0:1]
        ug = u * s.vec[3:4, :]
        grad = r * (ug - jnp.mean(ug, axis=1, keepdims=True) - n * jnp.mean(ug * n, axis=1, keepdims=True))
        low = grad.astype(BF)
        s.acc[rows, :] = grad
        s.gb[rows, :] = low
        s.vg[2:3, :] += jnp.sum(low.astype(F32), axis=0, keepdims=True)
        s.vg[3:4, :] += jnp.sum(u * n, axis=0, keepdims=True)
        s.vg[4:5, :] += jnp.sum(u, axis=0, keepdims=True)

    for g in range(3):
        up_chunk(g)
        rs_tick(2 + g)
        put_chunk((3 + g) % 4)
        rs_d(3 + g)

    gav = s.gb[...]
    s.fn[...] = dot_nt(gav, weight_row(0, 3)).astype(BF)
    rs_tick(5)

    s.o_ig[...] = s.ctx[...]
    for g in range(3):
        @pl.loop(0, 2)
        def _(j):
            lanes = pl.ds(pl.multiple_of(j * 128, 128), 128)
            q = s.qkv[0, g, :, lanes]
            k = s.qkv[1, g, :, lanes]
            v = s.qkv[2, g, :, lanes]
            go = s.fn[:, pl.ds(pl.multiple_of(g * 256 + j * 128, 128), 128)]
            gq = jnp.zeros((T, 128), F32)
            gk = jnp.zeros((T, 128), F32)
            gvv = jnp.zeros((T, 128), F32)
            for h in range(2):
                goh = head_only(go, h)
                w = s.p[4 * g + 2 * j + h]
                wf = w.astype(F32)
                dw = dot_nt(goh, v)
                ds = (wf * (dw - jnp.sum(wf * dw, axis=1, keepdims=True))).astype(BF)
                gq = gq + dot(ds, head_only(k, h))
                gk = gk + dot_tn(ds, head_only(q, h))
                gvv = gvv + dot_tn(w, goh)
            s.qkv[0, g, :, lanes] = (gq * 0.125).astype(BF)
            s.qkv[1, g, :, lanes] = (gk * 0.125).astype(BF)
            s.qkv[2, g, :, lanes] = gvv.astype(BF)

        if g == 0:
            rs_tick(6)
            rs_tick(7)
            rs_tick(8)
            rs_tick(9)
            greet(s.ready)
            pl.semaphore_wait(s.ready, len(partners))
        s.tr[...] = jnp.transpose(s.o_ig[...])
        v = dot(s.tr[...], s.gb[:, 256 * g : 256 * g + 256])
        s.act[3, 0:D] = v.astype(BF)
        s.tr[...] = jnp.transpose(s.x[...])
        for m in range(3):
            s.act[m, 0:D] = dot(s.tr[...], s.qkv[m, g]).astype(BF)
        for i, m in ((0, 0), (1, 2)):
            s.vg[i : i + 1, 256 * g : 256 * g + 256] = jnp.sum(s.qkv[m, g].astype(F32), axis=0, keepdims=True)
        put_chunk((6 + g) % 4)
        rs_d(6 + g)
        if g >= 1:
            rs_p1(5 + g)

    @pl.loop(0, 3)
    def _(m):
        s.acc[...] += dot_nt(jnp.concatenate([s.qkv[m, g] for g in range(3)], axis=1), weight_row(0, m))

    s.o_ig[...] = s.acc[...].astype(BF)
    rs_p2(6)
    rs_p1(8)
    rs_p2(7)
    rs_p3(6)
    rs_p2(8)
    rs_p3(7)
    rs_f(6)
    rs_p3(8)
    rs_f(7)
    rs_f(8)
    for j in range(6, 9):
        rs_done(j)

    def v_copy(src, dst, i, where):
        return copy(src, dst, s.vs.at[i], s.vr.at[i], where)

    half = pl.ds(pl.multiple_of((1 - C) * 8, 8), 8)
    mine = pl.ds(pl.multiple_of(C * 8, 8), 8)
    first = v_copy(s.vg.at[half], s.va.at[13], 14, sibling)
    first.start()
    first.wait()
    s.vo[0] = s.vg[mine, :] + s.va[13]
    axes = (
        (0, [device(X, Y, lax.rem(Z + d, 8), C) for d in range(1, 8)]),
        (1, [device(lax.rem(X + d, 4), Y, Z, C) for d in (1, 2, 3)]),
        (0, [device(X, lax.rem(Y + d, 4), Z, C) for d in (1, 2, 3)]),
    )
    sem_at = 0
    for which, peers in axes:
        moves = []
        for i, where in enumerate(peers):
            moves.append(v_copy(s.vo.at[which], s.va.at[sem_at + i], sem_at + i, where))
        for c in moves:
            c.start()
        for c in moves:
            c.wait()
        v = s.vo[which]
        for i in range(len(peers)):
            v = v + s.va[sem_at + i]
        s.vo[1 - which] = v
        sem_at += len(peers)
    s.vg[mine, :] = s.vo[1]
    last = v_copy(s.vo.at[1], s.vo.at[2], 13, sibling)
    last.start()
    last.wait()
    s.vg[half, :] = s.vo[2]

    for g in range(3):
        lo = 256 * g
        v = s.fin[6 + g]
        for m in range(3):
            s.o_qkv[:, m * D + lo : m * D + lo + 256] = v[12 * m : 12 * m + 12]
        s.o_wout[:, lo : lo + 256] = v[36:48]
        v = s.fin[3 + g]
        for m in range(4):
            s.o_up[:, m * D + lo : m * D + lo + 256] = v[12 * m : 12 * m + 12]
        s.o_down[:, lo : lo + 256] = s.fin[g]
    vg = s.vg[...]
    lane_f = lax.broadcasted_iota(jnp.int32, (D, 128), 0)
    lane_r = lax.broadcasted_iota(jnp.int32, (D, 128), 1)
    pick = jnp.logical_and(lane_f - 12 * fs == lane_r, lane_r < 12).astype(F32)
    pick_up = jnp.logical_and(lane_f - 48 * lax.rem(fs, 16) == lane_r, lane_r < 48).astype(F32)
    exact = functools.partial(
        lax.dot_general, dimension_numbers=(((1,), (0,)), ((), ())), precision=lax.Precision.HIGHEST,
        preferred_element_type=F32,
    )
    thin = exact(vg, pick)
    thin_up = exact(vg, pick_up)
    quarter = fs // 16
    row_i = lax.broadcasted_iota(jnp.int32, (16, 128), 0)
    up_row = jnp.sum(jnp.where(row_i == 8 + quarter, thin_up, 0.0), axis=0, keepdims=True)
    s.o_vec[...] = jnp.where(row_i == 8, up_row, thin)


def body(
    inputs, segment_ids, cotangent, qkv_weight, query_bias, value_bias, out_weight, out_bias, attn_gain,
    attn_shift, up_weight, up_bias, down_weight, down_bias, ffn_gain, ffn_shift,
):
    row = lambda v: v.reshape(1, -1)
    vmem = pl.BlockSpec(memory_space=pltpu.VMEM)
    outs = pl.pallas_call(
        kernel,
        out_shape=(
            jax.ShapeDtypeStruct((T, D), BF),
            jax.ShapeDtypeStruct((T, D), BF),
            jax.ShapeDtypeStruct((12, 3 * D), F32),
            jax.ShapeDtypeStruct((12, D), F32),
            jax.ShapeDtypeStruct((12, FF), F32),
            jax.ShapeDtypeStruct((48, D), F32),
            jax.ShapeDtypeStruct((16, 128), F32),
        ),
        in_specs=[vmem] * len(INS),
        out_specs=(vmem,) * len(OUTS),
        scratch_shapes=[v for _, v in SCRATCH]
        + [pltpu.SemaphoreType.DMA(v) for _, v in SEMS]
        + [pltpu.SemaphoreType.REGULAR],
        compiler_params=pltpu.CompilerParams(
            collective_id=0, has_side_effects=True, vmem_limit_bytes=63 * 2**20
        ),
    )(
        inputs.reshape(T, D), segment_ids, cotangent.reshape(T, D), qkv_weight, row(query_bias),
        row(value_bias), out_weight, row(out_bias), row(attn_gain), row(attn_shift), up_weight,
        row(up_bias), down_weight, row(down_bias), row(ffn_gain), row(ffn_shift),
    )
    vec = outs[6]
    small = lambda i: vec[i, :12]
    return (
        outs[0].reshape(1, T, D), outs[1].reshape(1, T, D), outs[2], small(0), small(1), outs[3], small(2),
        small(3), small(4), outs[4], vec[8, :48], outs[5], small(5), small(6), small(7),
    )


def solution(mesh):
    pages = P(("dp", "fsdp"), None, None)
    mat = P("fsdp", None)
    v = P("fsdp")
    in_specs = (pages, P(("dp", "fsdp"), None), pages, mat, v, v, mat, v, v, v, mat, v, mat, v, v, v)
    out_specs = (pages, pages, mat, v, v, mat, v, v, v, mat, v, mat, v, v, v)
    return jax.shard_map(body, mesh=mesh, in_specs=in_specs, out_specs=out_specs, check_vma=False)
```

```python
import functools
import types

import jax
import jax.numpy as jnp
from jax import lax
from jax.experimental import pallas as pl
from jax.experimental.pallas import tpu as pltpu
from jax.sharding import PartitionSpec as P

T = 512
D = 768
FF = 3072
BF = jnp.bfloat16
F32 = jnp.float32
MESH = pl.DeviceIdType.MESH
BLOCK = (2, 4, 2, 4, 48, 256)

SCRATCH = (
    ("G", pltpu.VMEM((9,) + BLOCK, BF)),
    ("GV", pltpu.VMEM((2, 4, 2, 4, 16, 128), BF)),
    ("gr", pltpu.VMEM((4,) + BLOCK, BF)),
    ("rd", pltpu.VMEM((6, 4, 2, 4, 48, 256), BF)),
    ("r1", pltpu.VMEM((6, 3, 4, 2, 48, 256), BF)),
    ("r2", pltpu.VMEM((6, 7, 2, 48, 256), BF)),
    ("r3", pltpu.VMEM((6, 4, 48, 256), BF)),
    ("fin", pltpu.VMEM((9, 48, 256), F32)),
    ("qkv", pltpu.VMEM((3, 3, T, 256), BF)),
    ("p", pltpu.VMEM((12, T, T), BF)),
    ("mask", pltpu.VMEM((T, T), BF)),
    ("ctx", pltpu.VMEM((T, D), BF)),
    ("n1", pltpu.VMEM((T, D), F32)),
    ("rs1", pltpu.VMEM((T, 128), F32)),
    ("fn", pltpu.VMEM((T, D), BF)),
    ("act", pltpu.VMEM((4, 3 * T, 256), BF)),
    ("slope", pltpu.VMEM((4, T, D), BF)),
    ("acc", pltpu.VMEM((T, D), F32)),
    ("gb", pltpu.VMEM((T, D), BF)),
    ("tr", pltpu.VMEM((D, T), BF)),
    ("perm", pltpu.VMEM((192, 192), BF)),
    ("vec", pltpu.VMEM((16, D), F32)),
    ("ub", pltpu.VMEM((8, FF), F32)),
    ("vg", pltpu.VMEM((16, D), F32)),
    ("va", pltpu.VMEM((14, 8, D), F32)),
    ("vo", pltpu.VMEM((5, 8, D), F32)),
    ("la", pltpu.VMEM((14, 8, 256), F32)),
    ("lo", pltpu.VMEM((5, 8, 256), F32)),
    ("small", pltpu.VMEM((16, 128), F32)),
    ("x", pltpu.VMEM((T, D), BF)),
    ("ct", pltpu.VMEM((T, D), BF)),
    ("own", pltpu.VMEM((48, 256), F32)),
)
SEMS = (
    ("zs", (10, 7)), ("zr", (10, 4)), ("xs", (10, 3)), ("xr", (10, 3)),
    ("ys", (10, 2)), ("yr", (10, 2)), ("ds", (10,)), ("dr", (10,)),
    ("rds", (9,)), ("rdr", (9,)), ("p1s", (9, 3)), ("p1r", (9, 3)),
    ("p2s", (9, 4)), ("p2r", (9, 7)), ("p3s", (9, 4)), ("p3r", (9, 4)),
    ("fs", (9,)), ("fr", (9,)), ("vs", (30,)), ("vr", (30,)), ("ls", (2,)),
)
INS = (
    "x_hbm", "seg", "ct_hbm", "wqkv", "qb", "vb", "wout", "ob", "ag", "ash",
    "wup", "ub_in", "wdown", "db", "fg", "fsh",
)
OUTS = ("o_out", "o_ig", "o_qkv", "o_wout", "o_up", "o_down", "o_vec")


EVENTS = (
    ("31", "f0", "23", "32", "f1"),
    ("24", "x0", "33", "16", "f2", "25", "x1"),
    ("34", "17", "f3", "35", "x2", "26", "f4"),
)


def dot(a, b):
    return lax.dot_general(a, b, (((1,), (0,)), ((), ())), preferred_element_type=F32)


def dot_nt(a, b):
    return lax.dot_general(a, b, (((1,), (1,)), ((), ())), preferred_element_type=F32)


def device(x, y, z, c):
    return ((y // 2) * 2 + c, z * 8 + lax.rem(y, 2) * 4 + x)


def kernel(*refs):
    names = INS + OUTS + tuple(n for n, _ in SCRATCH) + tuple(n for n, _ in SEMS) + ("ready",)
    s = types.SimpleNamespace(**dict(zip(names, refs, strict=True)))
    dp, fs = lax.axis_index("dp"), lax.axis_index("fsdp")
    C = lax.rem(dp, 2)
    YH = dp // 2
    Z = fs // 8
    YL = lax.rem(fs // 4, 2)
    X = lax.rem(fs, 4)
    Y = YH * 2 + YL
    ZT = Z // 4
    ZL = lax.rem(Z, 4)

    def copy(src, dst, send, recv, where):
        return pltpu.make_async_remote_copy(
            src_ref=src, dst_ref=dst, send_sem=send, recv_sem=recv, device_id=where, device_id_type=MESH
        )

    sibling = device(X, Y, Z, 1 - C)
    partners = (
        [sibling]
        + [device(lax.rem(X + d, 4), Y, Z, C) for d in (1, 2, 3)]
        + [device(X, lax.rem(Y + d, 4), Z, C) for d in (1, 2, 3)]
        + [device(X, Y, lax.rem(Z + d, 8), C) for d in range(1, 8)]
        + [device(lax.rem(X + d, 4), lax.rem(Y + 2, 4), Z, C) for d in (1, 2, 3)]
    )

    def greet(sem):
        for where in partners:
            pl.semaphore_signal(sem, inc=1, device_id=where, device_id_type=MESH)

    def gref(k):
        return s.GV if isinstance(k, int) and k == 9 else s.G.at[k]

    def z_copy(k, d):
        here = gref(k).at[ZT, ZL, YL, X]
        return copy(here, here, s.zs.at[k, d - 1], s.zr.at[k, ZL], device(X, Y, lax.rem(Z + d, 8), C))

    def z_recv(k, zl):
        here = gref(k).at[C, zl, YL, X]
        return copy(here, here, s.zs.at[k, 0], s.zr.at[k, zl], sibling)

    def x_copy(k, d):
        here = gref(k).at[C, :, YL, X]
        return copy(here, here, s.xs.at[k, d - 1], s.xr.at[k, d - 1], device(lax.rem(X + d, 4), Y, Z, C))

    def y_copy(k, i):
        here = gref(k).at[C, :, YL, pl.ds(2 * i, 2)]
        return copy(here, here, s.ys.at[k, i], s.yr.at[k, i], device(X, lax.rem(Y + 1 + 2 * i, 4), Z, C))

    def d_copy(k):
        here = gref(k).at[C]
        return copy(here, here, s.ds.at[k], s.dr.at[k], sibling)

    def ag_z(k):
        @pl.when(C == ZT)
        def _():
            for d in (4, 3, 5, 2, 6, 1, 7):
                z_copy(k, d).start()

    def ag_x(k):
        for zl in range(4):
            @pl.when(jnp.logical_or(C != ZT, zl != ZL))
            def _():
                z_recv(k, zl).wait_recv()
        for d in (2, 1, 3):
            x_copy(k, d).start()

    def ag_y(k):
        for d in (1, 2, 3):
            x_copy(k, d).wait_recv()
        for i in (0, 1):
            y_copy(k, i).start()

    def ag_d(k):
        for i in (0, 1):
            y_copy(k, i).wait_recv()
        d_copy(k).start()

    def ag_done(k):
        d_copy(k).wait()
        @pl.when(C == ZT)
        def _():
            for d in range(1, 8):
                z_copy(k, d).wait_send()
        for d in (1, 2, 3):
            x_copy(k, d).wait_send()
        for i in (0, 1):
            y_copy(k, i).wait_send()

    def ag_tick(t):
        for lag, step in ((4, ag_d), (2, ag_y), (0, ag_x)):
            if t == lag:
                step(9)
            if 0 <= t - lag <= 8:
                step(t - lag)

    barrier = pltpu.get_barrier_semaphore()
    greet(barrier)
    load_x = pltpu.make_async_copy(s.x_hbm, s.x, s.ls.at[0])
    load_x.start()
    load_ct = pltpu.make_async_copy(s.ct_hbm, s.ct, s.ls.at[1])
    load_ct.start()

    def own_block(k, parts):
        for m, part in enumerate(parts):
            s.own[12 * m : 12 * m + 12, :] = part.astype(F32)
        s.G[k, ZT, ZL, YL, X] = s.own[...].astype(BF)

    @pl.when(C == ZT)
    def _():
        for g in range(3):
            lo = 256 * g
            own_block(g, [s.wqkv[:, m * D + lo : m * D + lo + 256] for m in range(3)] + [s.wout[:, lo : lo + 256]])
        for g in range(3):
            lo = 256 * g
            own_block(3 + g, [s.wup[:, m * D + lo : m * D + lo + 256] for m in range(4)])
            s.G[6 + g, ZT, ZL, YL, X] = s.wdown[:, lo : lo + 256]
        s.small[...] = jnp.zeros((16, 128), F32)
        for i, v in enumerate((s.qb, s.vb, s.ob, s.ag, s.ash, s.db, s.fg, s.fsh)):
            s.small[i : i + 1, 0:12] = v[...].astype(F32)
        s.small[8:9, 0:48] = s.ub_in[...].astype(F32)
        s.GV[ZT, ZL, YL, X] = s.small[...].astype(BF)

    pl.semaphore_wait(barrier, len(partners))

    ag_z(9)
    for k in range(9):
        ag_z(k)

    row = lax.broadcasted_iota(jnp.int32, (192, 192), 0)
    col = lax.broadcasted_iota(jnp.int32, (192, 192), 1)
    swapped = lax.rem(row // 12, 4) * 48 + (row // 48) * 12 + lax.rem(row, 12)
    s.perm[...] = (col == swapped).astype(F32).astype(BF)
    segf = jnp.broadcast_to(s.seg[...].astype(F32), (128, T))
    seg_col = jnp.transpose(segf)[:, 0:1]
    s.mask[...] = jnp.where(seg_col == segf[0:1, :], 0.0, -1e30).astype(BF)
    s.vg[...] = jnp.zeros((16, D), F32)

    def reorder(src, dst):
        @pl.loop(0, 16, unroll=4)
        def _(i):
            a, b, c = i // 8, lax.rem(i // 2, 4), lax.rem(i, 2)
            v = src[a, b, c].reshape(192, 256)
            w = dot(s.perm[...], v).astype(BF)
            dst[a, b, c] = w.reshape(4, 48, 256)

    def weight(k, m):
        return s.G[k, :, :, :, m].reshape(D, 256)

    def weight_row(base, m):
        return jnp.concatenate([weight(base + g, m) for g in range(3)], axis=1)

    def down_rows(m):
        parts = [s.G[6 + g, m // 2, pl.ds(2 * (m % 2), 2)].reshape(D, 256) for g in range(3)]
        return jnp.concatenate(parts, axis=1)

    def active(m):
        return jnp.concatenate([s.act[m, T * g : T * g + T] for g in range(3)], axis=1)

    for t in range(5):
        ag_tick(t)
    ag_done(9)
    load_x.wait()

    pick_r = lax.broadcasted_iota(jnp.int32, (128, D), 0)
    pick_c = lax.broadcasted_iota(jnp.int32, (128, D), 1)
    s.vec[...] = jnp.zeros((16, D), F32)
    s.ub[...] = jnp.zeros((8, FF), F32)

    @pl.loop(0, 8, unroll=2)
    def _(i):
        gv = s.GV[i // 4, lax.rem(i, 4)].reshape(128, 128)
        wide = dot(gv, (lax.rem(pick_c, 12) == pick_r).astype(F32).astype(BF))
        owner = lax.broadcasted_iota(jnp.int32, (128, D), 0) // 16 + 8 * i
        lane = lax.broadcasted_iota(jnp.int32, (128, D), 1) // 12
        s.vec[...] += jnp.sum(jnp.where(owner == lane, wide, 0.0).reshape(8, 16, D), axis=0)
        sel_r = lax.broadcasted_iota(jnp.int32, (8, 128), 0)
        sel_c = lax.broadcasted_iota(jnp.int32, (8, 128), 1)
        rows8 = dot((sel_c == 16 * sel_r + 8).astype(F32).astype(BF), gv).astype(BF)
        for m in range(4):
            up_c = pick_c + m * D
            wide_up = dot(rows8, (lax.rem(up_c, 48) == pick_r).astype(F32).astype(BF))
            own_r = lax.broadcasted_iota(jnp.int32, (8, D), 0) + 8 * i
            own_c = (lax.broadcasted_iota(jnp.int32, (8, D), 1) + m * D) // 48
            s.ub[:, m * D : m * D + D] += jnp.where(own_r == own_c, wide_up, 0.0)

    s.ub[0:1, :] = jnp.sum(s.ub[...], axis=0, keepdims=True)

    head_lane = lax.broadcasted_iota(jnp.int32, (1, 128), 1) // 64

    def head_only(v, h):
        return jnp.where(head_lane == h, v, jnp.zeros_like(v))

    for g in range(3):
        ag_done(g)
        reorder(s.G.at[g], s.G.at[g])
        xv = s.x[...]
        for m in range(3):
            v = dot(xv, weight(g, m))
            if m != 1:
                i = 0 if m == 0 else 1
                v = v + s.vec[i : i + 1, 256 * g : 256 * g + 256]
            s.qkv[m, g] = v.astype(BF)
        if g < 2:
            ag_tick(5 + 2 * g)
        else:
            ag_tick(8)

        @pl.loop(0, 2)
        def _(j):
            lanes = pl.ds(pl.multiple_of(j * 128, 128), 128)
            q = s.qkv[0, g, :, lanes] * 0.125
            k = s.qkv[1, g, :, lanes]
            v = s.qkv[2, g, :, lanes]
            vt = jnp.transpose(v)
            outs = []
            for h in range(2):
                sc = dot_nt(head_only(k, h), q) + s.mask[...].astype(F32)
                e = jnp.exp(sc - jnp.max(sc, axis=0, keepdims=True))
                w = (e * (1.0 / jnp.sum(e, axis=0, keepdims=True))).astype(BF)
                s.p[4 * g + 2 * j + h] = w
                outs.append(dot(vt[64 * h : 64 * h + 64], w))
            out = jnp.transpose(jnp.concatenate(outs, axis=0).astype(BF))
            s.ctx[:, pl.ds(pl.multiple_of(g * 256 + j * 128, 128), 128)] = out

        if g == 0:
            ag_tick(6)

    ag_tick(9)
    cv = s.ctx[...]
    for g in range(3):
        s.acc[:, 256 * g : 256 * g + 256] = dot(cv, weight(g, 3))
    ag_tick(10)

    @pl.loop(0, 16, unroll=4)
    def _(i):
        rows = pl.ds(pl.multiple_of(i * 32, 32), 32)
        v = s.acc[rows, :] + s.vec[2:3, :] + s.x[rows, :].astype(F32)
        v = v - jnp.mean(v, axis=1, keepdims=True)
        r = lax.rsqrt(jnp.mean(v * v, axis=1, keepdims=True) + 1e-12)
        n = v * r
        s.n1[rows, :] = n
        s.rs1[rows, :] = jnp.broadcast_to(r, (32, 128))
        s.fn[rows, :] = (n * s.vec[3:4, :] + s.vec[4:5, :]).astype(BF)

    fv = s.fn[...]
    for g in range(3):
        if g:
            ag_tick(10 + g)
        ag_done(3 + g)
        reorder(s.G.at[3 + g], s.G.at[3 + g])
        for m in range(4):
            lo = 256 * g
            u = dot(fv, weight(3 + g, m)) + s.ub[0:1, m * D + lo : m * D + lo + 256]
            half = 0.5 * (1.0 + lax.erf(u * 0.7071067811865476))
            s.act[m, T * g : T * g + T] = (u * half).astype(BF)
            s.slope[m, :, lo : lo + 256] = (half + u * jnp.exp(-0.5 * u * u) * 0.3989422804014327).astype(BF)
    load_ct.wait()
    for g in range(3):
        ag_done(6 + g)
        lo = 256 * g
        total = jnp.zeros((T, 256), F32)
        for m in range(4):
            total = total + dot(active(m), s.G[6 + g, m // 2, 2 * (m % 2) : 2 * (m % 2) + 2].reshape(D, 256))
        s.acc[:, lo : lo + 256] = total

    @pl.loop(0, 16, unroll=4)
    def _(i):
        rows = pl.ds(pl.multiple_of(i * 32, 32), 32)
        v = s.acc[rows, :] + s.vec[5:6, :] + s.fn[rows, :].astype(F32)
        v = v - jnp.mean(v, axis=1, keepdims=True)
        r = lax.rsqrt(jnp.mean(v * v, axis=1, keepdims=True) + 1e-12)
        n = v * r
        gain = s.vec[6:7, :]
        s.o_out[rows, :] = (n * gain + s.vec[7:8, :]).astype(BF)
        u = s.ct[rows, :].astype(F32)
        ug = u * gain
        un = u * n
        grad = r * (ug - jnp.mean(ug, axis=1, keepdims=True) - n * jnp.mean(ug * n, axis=1, keepdims=True))
        low = grad.astype(BF)
        s.acc[rows, :] = grad
        s.gb[rows, :] = low
        s.vg[5:6, :] += jnp.sum(low.astype(F32), axis=0, keepdims=True)
        s.vg[6:7, :] += jnp.sum(un, axis=0, keepdims=True)
        s.vg[7:8, :] += jnp.sum(u, axis=0, keepdims=True)

    def rd(j):
        return s.rd.at[j] if j < 6 else s.G.at[j, 0]

    def r1(j, d):
        return s.r1.at[j, d] if j < 6 else s.G.at[j, 1, :, :, d]

    def r2(j, slot):
        return s.r2.at[j, slot] if j < 6 else s.G.at[j - 3, slot // 4, lax.rem(slot, 4), :, 0]

    def r3(j, slot):
        return s.r3.at[j, slot] if j < 6 else s.G.at[j - 3, 0, slot, 0, 1]

    def rd_copy(j):
        return copy(
            s.gr.at[j % 4, 1 - C], rd(j), s.rds.at[j], s.rdr.at[j], sibling
        )

    def p1_copy(j, d, c):
        if c == 0:
            xx = lax.rem(X + d, 4)
            src, where = s.gr.at[j % 4, 0, :, :, xx], device(xx, Y, Z, 0)
        else:
            yy = lax.rem(Y + d, 4)
            src = s.gr.at[j % 4, 1, :, lax.rem(yy, 2), pl.ds(2 * (yy // 2), 2)]
            where = device(X, yy, Z, 1)
        return copy(src, r1(j, d - 1), s.p1s.at[j, d - 1], s.p1r.at[j, d - 1], where)

    def p2_copy(j, zl):
        zz = C * 4 + zl
        slot = lax.rem(Z - zz + 8, 8) - 1
        return copy(
            r1(j, 0).at[zl], r2(j, slot), s.p2s.at[j, zl], s.p2r.at[j, slot],
            device(X, Y, zz, C),
        )

    def p2_recv(j, slot):
        return copy(
            r1(j, 0).at[0], r2(j, slot), s.p2s.at[j, 0], s.p2r.at[j, slot], sibling
        )

    def p3_copy0(j, d):
        yy = lax.rem(Y + d, 4)
        return copy(
            r2(j, 0).at[lax.rem(yy, 2)], r3(j, Y), s.p3s.at[j, d], s.p3r.at[j, Y],
            device(X, yy, Z, 0),
        )

    def p3_copy1(j, i, other):
        xx = 2 * YH + i
        yy = lax.rem(Y + 2 * other, 4)
        return copy(
            r2(j, 0).at[i], r3(j, X), s.p3s.at[j, 2 * i + other], s.p3r.at[j, X],
            device(xx, yy, Z, 1),
        )

    def p3_recv(j, slot):
        return copy(
            r2(j, 0).at[0], r3(j, slot), s.p3s.at[j, 0], s.p3r.at[j, slot], sibling
        )

    def f_copy(j):
        here = s.fin.at[j]
        return copy(here, here, s.fs.at[j], s.fr.at[j], sibling)

    def rs_d(j):
        rd_copy(j).start()

    def rs_p1(j):
        rd_copy(j).wait()

        @pl.loop(0, 8, unroll=2)
        def _(i):
            a, b = i // 2, lax.rem(i, 2)
            v = s.gr[j % 4, C, a, b].astype(F32) + rd(j)[a, b].astype(F32)
            s.gr[j % 4, C, a, b] = v.astype(BF)

        for c in (0, 1):
            @pl.when(C == c)
            def _():
                for d in (2, 1, 3):
                    p1_copy(j, d, c).start()

    def rs_p2(j):
        for c in (0, 1):
            @pl.when(C == c)
            def _():
                for d in (1, 2, 3):
                    p1_copy(j, d, c).wait()

        @pl.loop(0, 8, unroll=2)
        def _(i):
            a, b = i // 2, lax.rem(i, 2)
            mine = s.gr[j % 4, C, a, jnp.where(C == 0, b, YL), jnp.where(C == 0, X, 2 * YH + b)]
            v = mine.astype(F32)
            for d in range(3):
                v = v + r1(j, d)[a, b].astype(F32)
            r1(j, 0)[a, b] = v.astype(BF)

        for zl in range(4):
            @pl.when(C * 4 + zl != Z)
            def _():
                p2_copy(j, zl).start()

    def rs_p3(j):
        @pl.when(C == ZT)
        def _():
            for slot in range(7):
                p2_recv(j, slot).wait_recv()
            for b in range(2):
                v = r1(j, 0)[ZL, b].astype(F32)
                for slot in range(7):
                    v = v + r2(j, slot)[b].astype(F32)
                r2(j, 0)[b] = v.astype(BF)

        @pl.when(jnp.logical_and(C == 0, ZT == 0))
        def _():
            for d in (1, 2, 3):
                p3_copy0(j, d).start()

        @pl.when(jnp.logical_and(C == 1, ZT == 1))
        def _():
            for i in range(2):
                p3_copy1(j, i, 1).start()

                @pl.when(X != 2 * YH + i)
                def _():
                    p3_copy1(j, i, 0).start()

    def rs_f(j):
        own_slot = jnp.where(C == 0, Y, X)
        has_own = jnp.logical_or(C == 0, YH == X // 2)

        @pl.when(C == ZT)
        def _():
            @pl.when(has_own)
            def _():
                r3(j, own_slot)[...] = r2(j, 0)[jnp.where(C == 0, YL, lax.rem(X, 2))]
            for slot in range(4):
                @pl.when(jnp.logical_not(jnp.logical_and(has_own, own_slot == slot)))
                def _():
                    p3_recv(j, slot).wait_recv()
            v = r3(j, 0)[...].astype(F32)
            for slot in range(1, 4):
                v = v + r3(j, slot)[...].astype(F32)
            s.fin[j] = v
            f_copy(j).start()

    def rs_done(j):
        for zl in range(4):
            @pl.when(C * 4 + zl != Z)
            def _():
                p2_copy(j, zl).wait_send()

        @pl.when(jnp.logical_and(C == 0, ZT == 0))
        def _():
            for d in (1, 2, 3):
                p3_copy0(j, d).wait_send()

        @pl.when(jnp.logical_and(C == 1, ZT == 1))
        def _():
            for i in range(2):
                p3_copy1(j, i, 1).wait_send()

                @pl.when(X != 2 * YH + i)
                def _():
                    p3_copy1(j, i, 0).wait_send()

        @pl.when(C == ZT)
        def _():
            f_copy(j).wait_send()

        @pl.when(C != ZT)
        def _():
            f_copy(j).wait_recv()

    stages = {"d": rs_d, "1": rs_p1, "2": rs_p2, "3": rs_p3, "f": rs_f, "x": rs_done}

    def rs(*events):
        for e in events:
            stages[e[0]](int(e[1]))

    half = pl.ds(pl.multiple_of((1 - C) * 8, 8), 8)
    mine = pl.ds(pl.multiple_of(C * 8, 8), 8)
    axes = (
        [device(X, Y, lax.rem(Z + d, 8), C) for d in range(1, 8)],
        [device(lax.rem(X + d, 4), Y, Z, C) for d in (1, 2, 3)],
        [device(X, lax.rem(Y + d, 4), Z, C) for d in (1, 2, 3)],
    )
    starts = (1, 8, 11)

    def v_moves(late, step):
        held, got = (s.lo, s.la) if late else (s.vo, s.va)
        base = 15 if late else 0

        def move(src, dst, i, where):
            return copy(src, dst, s.vs.at[base + i], s.vr.at[base + i], where)

        if step == 0:
            return [move(held.at[4] if late else s.vg.at[half], got.at[0], 0, sibling)]
        if step == 4:
            return [move(held.at[3], held.at[4], 14, sibling)]
        first = starts[step - 1]
        return [move(held.at[step - 1], got.at[first + i], first + i, where) for i, where in enumerate(axes[step - 1])]

    def v_step(late, step):
        held, got = (s.lo, s.la) if late else (s.vo, s.va)
        if step:
            for c in v_moves(late, step - 1):
                c.wait()
        if step == 1:
            held[0] = (held[4] if late else s.vg[mine, :]) + got[0]
        elif 2 <= step <= 4:
            first = starts[step - 2]
            v = held[step - 2]
            for i in range(len(axes[step - 2])):
                v = v + got[first + i]
            held[step - 1] = v
        if step < (4 if late else 5):
            for c in v_moves(late, step):
                c.start()

    gbv = s.gb[...]
    for m in range(4):
        s.tr[...] = jnp.transpose(active(m))
        for g in range(3):
            v = dot(s.tr[...], gbv[:, 256 * g : 256 * g + 256])
            s.gr[g, m // 2, 2 * (m % 2) : 2 * (m % 2) + 2] = v.astype(BF).reshape(2, 2, 4, 48, 256)
    rs("d0", "d1", "d2")
    for m in range(4):
        low = (dot_nt(gbv, down_rows(m)) * s.slope[m].astype(F32)).astype(BF)
        s.slope[m] = low
        s.vg[8 + m : 9 + m, :] = jnp.sum(low.astype(F32), axis=0, keepdims=True)
    rs("10", "11", "12")
    @pl.loop(0, 4)
    def _(m):
        s.acc[...] += dot_nt(s.slope[m], weight_row(3, m))

    greet(s.ready)
    s.tr[...] = jnp.transpose(s.fn[...])

    def up_chunk(g):
        for m in range(4):
            v = dot(s.tr[...], s.slope[m, :, 256 * g : 256 * g + 256])
            s.act[m, 0:D] = v.astype(BF)

    def put_chunk(slot, last=(3, 0)):
        @pl.loop(0, 16, unroll=4)
        def _(i):
            a, b, c = i // 8, lax.rem(i // 2, 4), lax.rem(i, 2)
            at = pl.multiple_of(48 * i, 16)
            parts = [s.act[m, pl.ds(at, 48)] for m in range(3)]
            v = jnp.concatenate(parts + [s.act[last[0], pl.ds(at + last[1], 48)]], axis=0)
            s.gr[slot, a, b, c] = dot(s.perm[...], v).astype(BF).reshape(4, 48, 256)

    up_chunk(0)
    put_chunk(3)
    rs("d3")

    @pl.loop(0, 16, unroll=4)
    def _(i):
        rows = pl.ds(pl.multiple_of(i * 32, 32), 32)
        u = s.acc[rows, :]
        n = s.n1[rows, :]
        r = s.rs1[rows, 0:1]
        ug = u * s.vec[3:4, :]
        grad = r * (ug - jnp.mean(ug, axis=1, keepdims=True) - n * jnp.mean(ug * n, axis=1, keepdims=True))
        low = grad.astype(BF)
        s.acc[rows, :] = grad
        s.gb[rows, :] = low
        s.vg[2:3, :] += jnp.sum(low.astype(F32), axis=0, keepdims=True)
        s.vg[3:4, :] += jnp.sum(u * n, axis=0, keepdims=True)
        s.vg[4:5, :] += jnp.sum(u, axis=0, keepdims=True)

    rs("20", "13")
    up_chunk(1)
    put_chunk(0)
    rs("d4", "21", "30")
    up_chunk(2)
    put_chunk(1)
    rs("d5", "14")
    gav = s.gb[...]
    s.fn[...] = dot_nt(gav, weight_row(0, 3)).astype(BF)
    v_step(False, 0)
    s.tr[...] = jnp.transpose(s.ctx[...])
    out_at = ((3, 0), (3, D), (2, D))
    for g in range(3):
        m, at = out_at[g]
        s.act[m, at : at + D] = dot(s.tr[...], gav[:, 256 * g : 256 * g + 256]).astype(BF)
    s.tr[...] = jnp.transpose(s.x[...])
    s.lo[4] = jnp.zeros((8, 256), F32)
    rs("15", "22")

    for g in range(3):
        @pl.loop(0, 2)
        def _(j):
            lanes = pl.ds(pl.multiple_of(j * 128, 128), 128)
            q = s.qkv[0, g, :, lanes]
            k = s.qkv[1, g, :, lanes]
            v = s.qkv[2, g, :, lanes]
            go = s.fn[:, pl.ds(pl.multiple_of(g * 256 + j * 128, 128), 128)]
            kt = jnp.transpose(k)
            gk = jnp.zeros((T, 128), F32)
            gvv = jnp.zeros((T, 128), F32)
            gqs = []
            for h in range(2):
                w = s.p[4 * g + 2 * j + h]
                wf = w.astype(F32)
                dw = dot_nt(head_only(v, h), go)
                ds = (wf * (dw - jnp.sum(wf * dw, axis=0, keepdims=True))).astype(BF)
                gqs.append(dot(kt[64 * h : 64 * h + 64], ds))
                gk = gk + dot(ds, head_only(q, h))
                gvv = gvv + dot(w, head_only(go, h))
            gq = (jnp.concatenate(gqs, axis=0) * 0.125).astype(BF)
            s.qkv[0, g, :, lanes] = jnp.transpose(gq)
            s.qkv[1, g, :, lanes] = (gk * 0.125).astype(BF)
            s.qkv[2, g, :, lanes] = gvv.astype(BF)

        rs(*EVENTS[g])
        v_step(False, 1 + g)
        if g == 0:
            pl.semaphore_wait(s.ready, len(partners))
        for m in range(3):
            s.act[m, 0:D] = dot(s.tr[...], s.qkv[m, g]).astype(BF)
        for i, m in ((g, 0), (3 + g, 2)):
            s.lo[4, i : i + 1, :] = jnp.sum(s.qkv[m, g].astype(F32), axis=0, keepdims=True)
        put_chunk((6 + g) % 4, out_at[g])
        rs("d%d" % (6 + g))

    v_step(True, 0)
    v_step(False, 4)
    @pl.loop(0, 3)
    def _(m):
        s.acc[...] += dot_nt(jnp.concatenate([s.qkv[m, g] for g in range(3)], axis=1), weight_row(0, m))

    s.o_ig[...] = s.acc[...].astype(BF)
    v_step(True, 1)
    rs("27", "18", "x3", "f5", "36")
    v_step(True, 2)
    rs("x4", "37", "x5", "f6", "28")
    v_step(False, 5)
    v_step(True, 3)
    rs("f7", "38", "x6")
    v_step(True, 4)
    rs("f8", "x7", "x8")

    s.vg[mine, :] = s.vo[3]
    s.vg[half, :] = s.vo[4]
    for g in range(3):
        s.vg[0:1, 256 * g : 256 * g + 256] = s.lo[3, g : g + 1, :]
        s.vg[1:2, 256 * g : 256 * g + 256] = s.lo[3, 3 + g : 4 + g, :]
    for g in range(3):
        lo = 256 * g
        v = s.fin[6 + g]
        for m in range(3):
            s.o_qkv[:, m * D + lo : m * D + lo + 256] = v[12 * m : 12 * m + 12]
        s.o_wout[:, lo : lo + 256] = v[36:48]
        v = s.fin[3 + g]
        for m in range(4):
            s.o_up[:, m * D + lo : m * D + lo + 256] = v[12 * m : 12 * m + 12]
        s.o_down[:, lo : lo + 256] = s.fin[g]
    vg = s.vg[...]
    lane_f = lax.broadcasted_iota(jnp.int32, (D, 128), 0)
    lane_r = lax.broadcasted_iota(jnp.int32, (D, 128), 1)
    pick = jnp.logical_and(lane_f - 12 * fs == lane_r, lane_r < 12).astype(F32)
    pick_up = jnp.logical_and(lane_f - 48 * lax.rem(fs, 16) == lane_r, lane_r < 48).astype(F32)
    exact = functools.partial(
        lax.dot_general, dimension_numbers=(((1,), (0,)), ((), ())), precision=lax.Precision.HIGHEST,
        preferred_element_type=F32,
    )
    thin = exact(vg, pick)
    thin_up = exact(vg, pick_up)
    quarter = fs // 16
    row_i = lax.broadcasted_iota(jnp.int32, (16, 128), 0)
    up_row = jnp.sum(jnp.where(row_i == 8 + quarter, thin_up, 0.0), axis=0, keepdims=True)
    s.o_vec[...] = jnp.where(row_i == 8, up_row, thin)


VECTORS = ((0, 12), (1, 12), (2, 12), (3, 12), (4, 12), (8, 48), (5, 12), (6, 12), (7, 12))


def finish(*refs):
    whole, vec, results, thin = refs[:6], refs[6], refs[7:13], refs[13:22]
    held, sems = refs[22:28], refs[28]
    ins = [pltpu.make_async_copy(a, b, sems.at[0, i]) for i, (a, b) in enumerate(zip(whole, held))]
    outs = [pltpu.make_async_copy(a, b, sems.at[1, i]) for i, (a, b) in enumerate(zip(held, results))]
    for c in ins:
        c.start()
    for (i, n), ref in zip(VECTORS, thin):
        ref[...] = vec[i : i + 1, 0:n]
    for a, b in zip(ins, outs):
        a.wait()
        b.start()
    for c in outs:
        c.wait()


def body(
    inputs, segment_ids, cotangent, qkv_weight, query_bias, value_bias, out_weight, out_bias, attn_gain,
    attn_shift, up_weight, up_bias, down_weight, down_bias, ffn_gain, ffn_shift,
):
    row = lambda v: v.reshape(1, -1)
    vmem = pl.BlockSpec(memory_space=pltpu.VMEM)
    hbm = pl.BlockSpec(memory_space=pl.ANY)
    whole = (
        jax.ShapeDtypeStruct((T, D), BF),
        jax.ShapeDtypeStruct((T, D), BF),
        jax.ShapeDtypeStruct((12, 3 * D), F32),
        jax.ShapeDtypeStruct((12, D), F32),
        jax.ShapeDtypeStruct((12, FF), F32),
        jax.ShapeDtypeStruct((48, D), F32),
    )
    outs = pl.pallas_call(
        kernel,
        out_shape=whole + (jax.ShapeDtypeStruct((16, 128), F32),),
        in_specs=[hbm if name.endswith("_hbm") else vmem for name in INS],
        out_specs=(vmem,) * len(OUTS),
        scratch_shapes=[v for _, v in SCRATCH]
        + [pltpu.SemaphoreType.DMA(v) for _, v in SEMS]
        + [pltpu.SemaphoreType.REGULAR],
        compiler_params=pltpu.CompilerParams(
            collective_id=0, has_side_effects=True, vmem_limit_bytes=63 * 2**20
        ),
    )(
        inputs.reshape(T, D), segment_ids, cotangent.reshape(T, D), qkv_weight, row(query_bias),
        row(value_bias), out_weight, row(out_bias), row(attn_gain), row(attn_shift), up_weight,
        row(up_bias), down_weight, row(down_bias), row(ffn_gain), row(ffn_shift),
    )
    r = pl.pallas_call(
        finish,
        out_shape=whole + tuple(jax.ShapeDtypeStruct((1, n), F32) for _, n in VECTORS),
        in_specs=[hbm] * 6 + [vmem],
        out_specs=(hbm,) * 6 + (vmem,) * 9,
        scratch_shapes=[pltpu.VMEM(a.shape, a.dtype) for a in whole] + [pltpu.SemaphoreType.DMA((2, 6))],
    )(*outs)
    v = [a.reshape(-1) for a in r[6:]]
    return (
        r[0].reshape(1, T, D), r[1].reshape(1, T, D), r[2], v[0], v[1], r[3], v[2], v[3], v[4], r[4], v[5],
        r[5], v[6], v[7], v[8],
    )


def solution(mesh):
    pages = P(("dp", "fsdp"), None, None)
    mat = P("fsdp", None)
    v = P("fsdp")
    in_specs = (pages, P(("dp", "fsdp"), None), pages, mat, v, v, mat, v, v, v, mat, v, mat, v, v, v)
    out_specs = (pages, pages, mat, v, v, mat, v, v, v, mat, v, mat, v, v, v)
    return jax.shard_map(body, mesh=mesh, in_specs=in_specs, out_specs=out_specs, check_vma=False)
```

```python
import functools
import types

import jax
import jax.numpy as jnp
from jax import lax
from jax.experimental import pallas as pl
from jax.experimental.pallas import tpu as pltpu
from jax.sharding import PartitionSpec as P

T = 512
D = 768
FF = 3072
BF = jnp.bfloat16
F32 = jnp.float32
MESH = pl.DeviceIdType.MESH
ROWS = 128
BLOCK = (2, 4, 2, 4, 48, 256)

SCRATCH = (
    ("G", pltpu.VMEM((9,) + BLOCK, BF)),
    ("GV", pltpu.VMEM((2, 4, 2, 4, 16, 128), BF)),
    ("gr", pltpu.VMEM((4,) + BLOCK, BF)),
    ("rd", pltpu.VMEM((6, 4, 2, 4, 48, 256), BF)),
    ("r1", pltpu.VMEM((6, 3, 4, 2, 48, 256), BF)),
    ("r2", pltpu.VMEM((6, 7, 2, 48, 256), BF)),
    ("r3", pltpu.VMEM((6, 4, 48, 256), BF)),
    ("fin", pltpu.VMEM((9, 48, 256), F32)),
    ("qkv", pltpu.VMEM((3, 3, T, 256), BF)),
    ("p", pltpu.VMEM((12, T, T), BF)),
    ("mask", pltpu.VMEM((T, T), BF)),
    ("ctx", pltpu.VMEM((T, D), BF)),
    ("n1", pltpu.VMEM((T, D), F32)),
    ("rs1", pltpu.VMEM((T, 128), F32)),
    ("fn", pltpu.VMEM((T, D), BF)),
    ("act", pltpu.VMEM((4, 3 * T, 256), BF)),
    ("slope", pltpu.VMEM((4, T, D), BF)),
    ("acc", pltpu.VMEM((T, D), F32)),
    ("gb", pltpu.VMEM((T, D), BF)),
    ("tr", pltpu.VMEM((D, T), BF)),
    ("perm", pltpu.VMEM((192, 192), BF)),
    ("vec", pltpu.VMEM((16, D), F32)),
    ("ub", pltpu.VMEM((8, FF), F32)),
    ("vg", pltpu.VMEM((16, D), F32)),
    ("va", pltpu.VMEM((14, 8, D), F32)),
    ("vo", pltpu.VMEM((5, 8, D), F32)),
    ("la", pltpu.VMEM((14, 8, 256), F32)),
    ("lo", pltpu.VMEM((5, 8, 256), F32)),
    ("vp", pltpu.VMEM((6, 8, D), F32)),
    ("small", pltpu.VMEM((16, 128), F32)),
    ("x", pltpu.VMEM((T, D), BF)),
    ("ct", pltpu.VMEM((T, D), BF)),
    ("own", pltpu.VMEM((48, 256), F32)),
)
SEMS = (
    ("zs", (10, 7)), ("zr", (10, 4)), ("xs", (10, 3)), ("xr", (10, 3)),
    ("ys", (10, 2)), ("yr", (10, 2)), ("ds", (10,)), ("dr", (10,)),
    ("rds", (9,)), ("rdr", (9,)), ("p1s", (9, 3)), ("p1r", (9, 3)),
    ("p2s", (9, 4)), ("p2r", (9, 7)), ("p3s", (9, 4)), ("p3r", (9, 4)),
    ("fs", (9,)), ("fr", (9,)), ("vs", (30,)), ("vr", (30,)), ("ls", (2,)),
)
INS = (
    "x_hbm", "seg", "ct_hbm", "wqkv", "qb", "vb", "wout", "ob", "ag", "ash",
    "wup", "ub_in", "wdown", "db", "fg", "fsh",
)
OUTS = ("o_out", "o_ig", "o_qkv", "o_wout", "o_up", "o_down", "o_vec")


EVENTS = (
    ("31", "f0", "23", "32"),
    ("24", "33", "16", "f1", "x0", "f2", "25"),
    ("34", "17", "f3", "35", "x1", "x2", "26"),
)


def dot(a, b):
    return lax.dot_general(a, b, (((1,), (0,)), ((), ())), preferred_element_type=F32)


def dot_nt(a, b):
    return lax.dot_general(a, b, (((1,), (1,)), ((), ())), preferred_element_type=F32)


def device(x, y, z, c):
    return ((y // 2) * 2 + c, z * 8 + lax.rem(y, 2) * 4 + x)


def kernel(*refs):
    names = INS + OUTS + tuple(n for n, _ in SCRATCH) + tuple(n for n, _ in SEMS) + ("ready",)
    s = types.SimpleNamespace(**dict(zip(names, refs, strict=True)))
    dp, fs = lax.axis_index("dp"), lax.axis_index("fsdp")
    C = lax.rem(dp, 2)
    YH = dp // 2
    Z = fs // 8
    YL = lax.rem(fs // 4, 2)
    X = lax.rem(fs, 4)
    Y = YH * 2 + YL
    ZT = Z // 4
    ZL = lax.rem(Z, 4)

    def copy(src, dst, send, recv, where):
        return pltpu.make_async_remote_copy(
            src_ref=src, dst_ref=dst, send_sem=send, recv_sem=recv, device_id=where, device_id_type=MESH
        )

    sibling = device(X, Y, Z, 1 - C)
    partners = (
        [sibling]
        + [device(lax.rem(X + d, 4), Y, Z, C) for d in (1, 2, 3)]
        + [device(X, lax.rem(Y + d, 4), Z, C) for d in (1, 2, 3)]
        + [device(X, Y, lax.rem(Z + d, 8), C) for d in range(1, 8)]
        + [device(lax.rem(X + d, 4), lax.rem(Y + 2, 4), Z, C) for d in (1, 2, 3)]
    )

    def greet(sem):
        for where in partners:
            pl.semaphore_signal(sem, inc=1, device_id=where, device_id_type=MESH)

    def gref(k):
        return s.GV if isinstance(k, int) and k == 9 else s.G.at[k]

    def z_copy(k, d):
        here = gref(k).at[ZT, ZL, YL, X]
        return copy(here, here, s.zs.at[k, d - 1], s.zr.at[k, ZL], device(X, Y, lax.rem(Z + d, 8), C))

    def z_recv(k, zl):
        here = gref(k).at[C, zl, YL, X]
        return copy(here, here, s.zs.at[k, 0], s.zr.at[k, zl], sibling)

    def x_copy(k, d):
        here = gref(k).at[C, :, YL, X]
        return copy(here, here, s.xs.at[k, d - 1], s.xr.at[k, d - 1], device(lax.rem(X + d, 4), Y, Z, C))

    def y_copy(k, i):
        here = gref(k).at[C, :, YL, pl.ds(2 * i, 2)]
        return copy(here, here, s.ys.at[k, i], s.yr.at[k, i], device(X, lax.rem(Y + 1 + 2 * i, 4), Z, C))

    def d_copy(k):
        here = gref(k).at[C]
        return copy(here, here, s.ds.at[k], s.dr.at[k], sibling)

    def last_x(d):
        here = s.G.at[8, ZT, ZL, YL, X]
        return copy(here, here, s.xs.at[8, d - 1], s.xr.at[8, d - 1], device(lax.rem(X + d, 4), Y, Z, C))

    def last_y(i):
        here = s.G.at[8, ZT, ZL, YL, pl.ds(2 * i, 2)]
        return copy(here, here, s.ys.at[8, i], s.yr.at[8, i], device(X, lax.rem(Y + 1 + 2 * i, 4), Z, C))

    def last_z(d):
        here = s.G.at[8, ZT, ZL]
        return copy(here, here, s.zs.at[8, d - 1], s.zr.at[8, ZL], device(X, Y, lax.rem(Z + d, 8), C))

    def last_got(zl):
        here = s.G.at[8, C, zl]
        return copy(here, here, s.zs.at[8, 0], s.zr.at[8, zl], sibling)

    def last_step(n):
        @pl.when(C == ZT)
        def _():
            if n == 0:
                for d in (2, 1, 3):
                    last_x(d).start()
            elif n == 1:
                for d in (1, 2, 3):
                    last_x(d).wait()
                for i in (0, 1):
                    last_y(i).start()
            elif n == 2:
                for i in (0, 1):
                    last_y(i).wait()
                for d in (4, 3, 5, 2, 6, 1, 7):
                    last_z(d).start()
            elif n == 4:
                for d in range(1, 8):
                    last_z(d).wait_send()

        if n == 3:
            for zl in range(4):
                @pl.when(jnp.logical_or(C != ZT, zl != ZL))
                def _():
                    last_got(zl).wait_recv()
            d_copy(8).start()
        elif n == 4:
            d_copy(8).wait()

    def ag_x(k):
        for zl in range(4):
            @pl.when(jnp.logical_or(C != ZT, zl != ZL))
            def _():
                z_recv(k, zl).wait_recv()
        for d in (2, 1, 3):
            x_copy(k, d).start()

    def ag_y(k):
        for d in (1, 2, 3):
            x_copy(k, d).wait_recv()
        for i in (0, 1):
            y_copy(k, i).start()

    def ag_d(k):
        for i in (0, 1):
            y_copy(k, i).wait_recv()
        d_copy(k).start()

    def ag_done(k):
        d_copy(k).wait()
        @pl.when(C == ZT)
        def _():
            for d in range(1, 8):
                z_copy(k, d).wait_send()
        for d in (1, 2, 3):
            x_copy(k, d).wait_send()
        for i in (0, 1):
            y_copy(k, i).wait_send()

    sends = {"x": ag_x, "y": ag_y, "d": ag_d, "l": last_step}

    def ag(*events):
        for e in events:
            if e in ("x0", "y0", "d0"):
                sends[e[0]](9)
            sends[e[0]](int(e[1]))

    barrier = pltpu.get_barrier_semaphore()
    greet(barrier)
    load_x = pltpu.make_async_copy(s.x_hbm, s.x, s.ls.at[0])
    load_x.start()
    load_ct = pltpu.make_async_copy(s.ct_hbm, s.ct, s.ls.at[1])
    load_ct.start()

    def own_block(k, parts):
        for m, part in enumerate(parts):
            s.own[12 * m : 12 * m + 12, :] = part.astype(F32)
        s.G[k, ZT, ZL, YL, X] = s.own[...].astype(BF)

    def pack(k):
        lo = 256 * (k % 3)
        if k < 3:
            own_block(k, [s.wqkv[:, m * D + lo : m * D + lo + 256] for m in range(3)] + [s.wout[:, lo : lo + 256]])
        elif k < 6:
            own_block(k, [s.wup[:, m * D + lo : m * D + lo + 256] for m in range(4)])
        else:
            s.G[k, ZT, ZL, YL, X] = s.wdown[:, lo : lo + 256]

    @pl.when(C == ZT)
    def _():
        pack(0)
        s.small[...] = jnp.zeros((16, 128), F32)
        for i, v in enumerate((s.qb, s.vb, s.ob, s.ag, s.ash, s.db, s.fg, s.fsh)):
            s.small[i : i + 1, 0:12] = v[...].astype(F32)
        s.small[8:9, 0:48] = s.ub_in[...].astype(F32)
        s.GV[ZT, ZL, YL, X] = s.small[...].astype(BF)

    pl.semaphore_wait(barrier, len(partners))

    @pl.when(C == ZT)
    def _():
        for k in (9, 0, 1, 2, 3, 4, 5, 6, 7, 8):
            if 1 <= k <= 8:
                pack(k)
            if k < 8 or k == 9:
                for d in (4, 3, 5, 2, 6, 1, 7):
                    z_copy(k, d).start()

    row = lax.broadcasted_iota(jnp.int32, (192, 192), 0)
    col = lax.broadcasted_iota(jnp.int32, (192, 192), 1)
    swapped = lax.rem(row // 12, 4) * 48 + (row // 48) * 12 + lax.rem(row, 12)
    s.perm[...] = (col == swapped).astype(F32).astype(BF)
    segf = jnp.broadcast_to(s.seg[...].astype(F32), (128, T))
    seg_col = jnp.transpose(segf)[:, 0:1]
    s.mask[...] = jnp.where(seg_col == segf[0:1, :], 0.0, -1e30).astype(BF)
    s.vg[...] = jnp.zeros((16, D), F32)
    s.vp[...] = jnp.zeros((6, 8, D), F32)

    def reorder(src, dst):
        @pl.loop(0, 16, unroll=4)
        def _(i):
            a, b, c = i // 8, lax.rem(i // 2, 4), lax.rem(i, 2)
            v = src[a, b, c].reshape(192, 256)
            w = dot(s.perm[...], v).astype(BF)
            dst[a, b, c] = w.reshape(4, 48, 256)

    def weight(k, m):
        return s.G[k, :, :, :, m].reshape(D, 256)

    def weight_row(base, m):
        return jnp.concatenate([weight(base + g, m) for g in range(3)], axis=1)

    def down_rows(m):
        parts = [s.G[6 + g, m // 2, pl.ds(2 * (m % 2), 2)].reshape(D, 256) for g in range(3)]
        return jnp.concatenate(parts, axis=1)

    def active(m):
        return jnp.concatenate([s.act[m, T * g : T * g + T] for g in range(3)], axis=1)

    ag("l0", "x0", "x1", "x2", "l1", "y0", "x3", "x4", "y1", "x5", "l2", "d0", "y2")
    ag_done(9)
    load_x.wait()
    load_ct.wait()

    pick_r = lax.broadcasted_iota(jnp.int32, (128, D), 0)
    pick_c = lax.broadcasted_iota(jnp.int32, (128, D), 1)
    s.vec[...] = jnp.zeros((16, D), F32)
    s.ub[...] = jnp.zeros((8, FF), F32)

    @pl.loop(0, 8, unroll=2)
    def _(i):
        gv = s.GV[i // 4, lax.rem(i, 4)].reshape(128, 128)
        wide = dot(gv, (lax.rem(pick_c, 12) == pick_r).astype(F32).astype(BF))
        owner = lax.broadcasted_iota(jnp.int32, (128, D), 0) // 16 + 8 * i
        lane = lax.broadcasted_iota(jnp.int32, (128, D), 1) // 12
        s.vec[...] += jnp.sum(jnp.where(owner == lane, wide, 0.0).reshape(8, 16, D), axis=0)
        sel_r = lax.broadcasted_iota(jnp.int32, (8, 128), 0)
        sel_c = lax.broadcasted_iota(jnp.int32, (8, 128), 1)
        rows8 = dot((sel_c == 16 * sel_r + 8).astype(F32).astype(BF), gv).astype(BF)
        for m in range(4):
            up_c = pick_c + m * D
            wide_up = dot(rows8, (lax.rem(up_c, 48) == pick_r).astype(F32).astype(BF))
            own_r = lax.broadcasted_iota(jnp.int32, (8, D), 0) + 8 * i
            own_c = (lax.broadcasted_iota(jnp.int32, (8, D), 1) + m * D) // 48
            s.ub[:, m * D : m * D + D] += jnp.where(own_r == own_c, wide_up, 0.0)

    s.ub[0:1, :] = jnp.sum(s.ub[...], axis=0, keepdims=True)

    head_lane = lax.broadcasted_iota(jnp.int32, (1, 128), 1) // 64

    def head_only(v, h):
        return jnp.where(head_lane == h, v, jnp.zeros_like(v))

    for g in range(3):
        ag_done(g)
        reorder(s.G.at[g], s.G.at[g])
        xv = s.x[...]
        for m in range(3):
            v = dot(xv, weight(g, m))
            if m != 1:
                i = 0 if m == 0 else 1
                v = v + s.vec[i : i + 1, 256 * g : 256 * g + 256]
            s.qkv[m, g] = v.astype(BF)
        ag(*(("d1", "y3", "x6", "x7"), ("d3",), ("y6",))[g])

        @pl.loop(0, 2)
        def _(j):
            lanes = pl.ds(pl.multiple_of(j * 128, 128), 128)
            q = s.qkv[0, g, :, lanes] * 0.125
            k = s.qkv[1, g, :, lanes]
            v = s.qkv[2, g, :, lanes]
            vt = jnp.transpose(v)
            outs = []
            for h in range(2):
                sc = dot_nt(head_only(k, h), q) + s.mask[...].astype(F32)
                e = jnp.exp(sc - jnp.max(sc, axis=0, keepdims=True))
                w = (e * (1.0 / jnp.sum(e, axis=0, keepdims=True))).astype(BF)
                s.p[4 * g + 2 * j + h] = w
                outs.append(dot(vt[64 * h : 64 * h + 64], w))
            out = jnp.transpose(jnp.concatenate(outs, axis=0).astype(BF))
            s.ctx[:, pl.ds(pl.multiple_of(g * 256 + j * 128, 128), 128)] = out

        ag(*(("d2", "y4"), ("y5", "d4"), ("d5", "y7"))[g])

    cv = s.ctx[...]
    for g in range(3):
        s.acc[:, 256 * g : 256 * g + 256] = dot(cv, weight(g, 3))

    @pl.loop(0, T // ROWS)
    def _(i):
        rows = pl.ds(pl.multiple_of(i * ROWS, ROWS), ROWS)
        v = s.acc[rows, :] + s.vec[2:3, :] + s.x[rows, :].astype(F32)
        v = v - jnp.mean(v, axis=1, keepdims=True)
        r = lax.rsqrt(jnp.mean(v * v, axis=1, keepdims=True) + 1e-12)
        n = v * r
        s.n1[rows, :] = n
        s.rs1[rows, :] = jnp.broadcast_to(r, (ROWS, 128))
        s.fn[rows, :] = (n * s.vec[3:4, :] + s.vec[4:5, :]).astype(BF)

    fv = s.fn[...]
    ag("d6")
    for g in range(3):
        if g == 1:
            ag("d7", "l3")
        ag_done(3 + g)
        reorder(s.G.at[3 + g], s.G.at[3 + g])
        for m in range(4):
            lo = 256 * g
            u = dot(fv, weight(3 + g, m)) + s.ub[0:1, m * D + lo : m * D + lo + 256]
            half = 0.5 * (1.0 + lax.erf(u * 0.7071067811865476))
            s.act[m, T * g : T * g + T] = (u * half).astype(BF)
            s.slope[m, :, lo : lo + 256] = (half + u * jnp.exp(-0.5 * u * u) * 0.3989422804014327).astype(BF)
    for g in range(3):
        if g < 2:
            ag_done(6 + g)
        else:
            last_step(4)
        lo = 256 * g
        total = jnp.zeros((T, 256), F32)
        for m in range(4):
            total = total + dot(active(m), s.G[6 + g, m // 2, 2 * (m % 2) : 2 * (m % 2) + 2].reshape(D, 256))
        s.acc[:, lo : lo + 256] = total

    def fold(i, v):
        s.vp[i] += jnp.sum(v.reshape(ROWS // 8, 8, D), axis=0)

    @pl.loop(0, T // ROWS)
    def _(i):
        rows = pl.ds(pl.multiple_of(i * ROWS, ROWS), ROWS)
        v = s.acc[rows, :] + s.vec[5:6, :] + s.fn[rows, :].astype(F32)
        v = v - jnp.mean(v, axis=1, keepdims=True)
        r = lax.rsqrt(jnp.mean(v * v, axis=1, keepdims=True) + 1e-12)
        n = v * r
        gain = s.vec[6:7, :]
        s.o_out[rows, :] = (n * gain + s.vec[7:8, :]).astype(BF)
        u = s.ct[rows, :].astype(F32)
        ug = u * gain
        un = u * n
        grad = r * (ug - jnp.mean(ug, axis=1, keepdims=True) - n * jnp.mean(ug * n, axis=1, keepdims=True))
        low = grad.astype(BF)
        s.acc[rows, :] = grad
        s.gb[rows, :] = low
        fold(3, low.astype(F32))
        fold(4, un)
        fold(5, u)

    def rd(j):
        return s.rd.at[j] if j < 6 else s.G.at[j, 0]

    def r1(j, d):
        return s.r1.at[j, d] if j < 6 else s.G.at[j, 1, :, :, d]

    def r2(j, slot):
        return s.r2.at[j, slot] if j < 6 else s.G.at[j - 3, slot // 4, lax.rem(slot, 4), :, 0]

    def r3(j, slot):
        return s.r3.at[j, slot] if j < 6 else s.G.at[j - 3, 0, slot, 0, 1]

    def rd_copy(j):
        return copy(
            s.gr.at[j % 4, 1 - C], rd(j), s.rds.at[j], s.rdr.at[j], sibling
        )

    def p1_copy(j, d, c):
        if c == 0:
            xx = lax.rem(X + d, 4)
            src, where = s.gr.at[j % 4, 0, :, :, xx], device(xx, Y, Z, 0)
        else:
            yy = lax.rem(Y + d, 4)
            src = s.gr.at[j % 4, 1, :, lax.rem(yy, 2), pl.ds(2 * (yy // 2), 2)]
            where = device(X, yy, Z, 1)
        return copy(src, r1(j, d - 1), s.p1s.at[j, d - 1], s.p1r.at[j, d - 1], where)

    def p2_copy(j, zl):
        zz = C * 4 + zl
        slot = lax.rem(Z - zz + 8, 8) - 1
        return copy(
            r1(j, 0).at[zl], r2(j, slot), s.p2s.at[j, zl], s.p2r.at[j, slot],
            device(X, Y, zz, C),
        )

    def p2_recv(j, slot):
        return copy(
            r1(j, 0).at[0], r2(j, slot), s.p2s.at[j, 0], s.p2r.at[j, slot], sibling
        )

    def p3_copy0(j, d):
        yy = lax.rem(Y + d, 4)
        return copy(
            r2(j, 0).at[lax.rem(yy, 2)], r3(j, Y), s.p3s.at[j, d], s.p3r.at[j, Y],
            device(X, yy, Z, 0),
        )

    def p3_copy1(j, i, other):
        xx = 2 * YH + i
        yy = lax.rem(Y + 2 * other, 4)
        return copy(
            r2(j, 0).at[i], r3(j, X), s.p3s.at[j, 2 * i + other], s.p3r.at[j, X],
            device(xx, yy, Z, 1),
        )

    def p3_recv(j, slot):
        return copy(
            r2(j, 0).at[0], r3(j, slot), s.p3s.at[j, 0], s.p3r.at[j, slot], sibling
        )

    def f_copy(j):
        here = s.fin.at[j]
        return copy(here, here, s.fs.at[j], s.fr.at[j], sibling)

    def rs_d(j):
        rd_copy(j).start()

    def rs_p1(j):
        rd_copy(j).wait()

        @pl.loop(0, 8, unroll=2)
        def _(i):
            a, b = i // 2, lax.rem(i, 2)
            v = s.gr[j % 4, C, a, b].astype(F32) + rd(j)[a, b].astype(F32)
            s.gr[j % 4, C, a, b] = v.astype(BF)

        for c in (0, 1):
            @pl.when(C == c)
            def _():
                for d in (2, 1, 3):
                    p1_copy(j, d, c).start()

    def rs_p2(j):
        for c in (0, 1):
            @pl.when(C == c)
            def _():
                for d in (1, 2, 3):
                    p1_copy(j, d, c).wait()

        @pl.loop(0, 8, unroll=2)
        def _(i):
            a, b = i // 2, lax.rem(i, 2)
            mine = s.gr[j % 4, C, a, jnp.where(C == 0, b, YL), jnp.where(C == 0, X, 2 * YH + b)]
            v = mine.astype(F32)
            for d in range(3):
                v = v + r1(j, d)[a, b].astype(F32)
            r1(j, 0)[a, b] = v.astype(BF)

        for zl in range(4):
            @pl.when(C * 4 + zl != Z)
            def _():
                p2_copy(j, zl).start()

    def rs_p3(j):
        @pl.when(C == ZT)
        def _():
            for slot in range(7):
                p2_recv(j, slot).wait_recv()
            for b in range(2):
                v = r1(j, 0)[ZL, b].astype(F32)
                for slot in range(7):
                    v = v + r2(j, slot)[b].astype(F32)
                r2(j, 0)[b] = v.astype(BF)

        @pl.when(jnp.logical_and(C == 0, ZT == 0))
        def _():
            for d in (1, 2, 3):
                p3_copy0(j, d).start()

        @pl.when(jnp.logical_and(C == 1, ZT == 1))
        def _():
            for i in range(2):
                p3_copy1(j, i, 1).start()

                @pl.when(X != 2 * YH + i)
                def _():
                    p3_copy1(j, i, 0).start()

    def rs_f(j):
        own_slot = jnp.where(C == 0, Y, X)
        has_own = jnp.logical_or(C == 0, YH == X // 2)

        @pl.when(C == ZT)
        def _():
            @pl.when(has_own)
            def _():
                r3(j, own_slot)[...] = r2(j, 0)[jnp.where(C == 0, YL, lax.rem(X, 2))]
            for slot in range(4):
                @pl.when(jnp.logical_not(jnp.logical_and(has_own, own_slot == slot)))
                def _():
                    p3_recv(j, slot).wait_recv()
            v = r3(j, 0)[...].astype(F32)
            for slot in range(1, 4):
                v = v + r3(j, slot)[...].astype(F32)
            s.fin[j] = v
            f_copy(j).start()

    def rs_done(j):
        for zl in range(4):
            @pl.when(C * 4 + zl != Z)
            def _():
                p2_copy(j, zl).wait_send()

        @pl.when(jnp.logical_and(C == 0, ZT == 0))
        def _():
            for d in (1, 2, 3):
                p3_copy0(j, d).wait_send()

        @pl.when(jnp.logical_and(C == 1, ZT == 1))
        def _():
            for i in range(2):
                p3_copy1(j, i, 1).wait_send()

                @pl.when(X != 2 * YH + i)
                def _():
                    p3_copy1(j, i, 0).wait_send()

        @pl.when(C == ZT)
        def _():
            f_copy(j).wait_send()

        @pl.when(C != ZT)
        def _():
            f_copy(j).wait_recv()

    stages = {"d": rs_d, "1": rs_p1, "2": rs_p2, "3": rs_p3, "f": rs_f, "x": rs_done}

    def rs(*events):
        for e in events:
            stages[e[0]](int(e[1]))

    half = pl.ds(pl.multiple_of((1 - C) * 8, 8), 8)
    mine = pl.ds(pl.multiple_of(C * 8, 8), 8)
    axes = (
        [device(X, Y, lax.rem(Z + d, 8), C) for d in range(1, 8)],
        [device(lax.rem(X + d, 4), Y, Z, C) for d in (1, 2, 3)],
        [device(X, lax.rem(Y + d, 4), Z, C) for d in (1, 2, 3)],
    )
    starts = (1, 8, 11)

    def v_moves(late, step):
        held, got = (s.lo, s.la) if late else (s.vo, s.va)
        base = 15 if late else 0

        def move(src, dst, i, where):
            return copy(src, dst, s.vs.at[base + i], s.vr.at[base + i], where)

        if step == 0:
            return [move(held.at[4] if late else s.vg.at[half], got.at[0], 0, sibling)]
        if step == 4:
            return [move(held.at[3], held.at[4], 14, sibling)]
        first = starts[step - 1]
        return [move(held.at[step - 1], got.at[first + i], first + i, where) for i, where in enumerate(axes[step - 1])]

    def v_step(late, step):
        held, got = (s.lo, s.la) if late else (s.vo, s.va)
        if step:
            for c in v_moves(late, step - 1):
                c.wait()
        if step == 1:
            held[0] = (held[4] if late else s.vg[mine, :]) + got[0]
        elif 2 <= step <= 4:
            first = starts[step - 2]
            v = held[step - 2]
            for i in range(len(axes[step - 2])):
                v = v + got[first + i]
            held[step - 1] = v
        if step < (4 if late else 5):
            for c in v_moves(late, step):
                c.start()

    gbv = s.gb[...]
    for m in range(4):
        s.tr[...] = jnp.transpose(active(m))
        for g in range(3):
            v = dot(s.tr[...], gbv[:, 256 * g : 256 * g + 256])
            s.gr[g, m // 2, 2 * (m % 2) : 2 * (m % 2) + 2] = v.astype(BF).reshape(2, 2, 4, 48, 256)
    rs("d0", "d1", "d2")
    for m in range(4):
        low = (dot_nt(gbv, down_rows(m)) * s.slope[m].astype(F32)).astype(BF)
        s.slope[m] = low
        s.vg[8 + m : 9 + m, :] = jnp.sum(low.astype(F32), axis=0, keepdims=True)
    rs("10", "11", "12")
    @pl.loop(0, 4)
    def _(m):
        s.acc[...] += dot_nt(s.slope[m], weight_row(3, m))

    greet(s.ready)
    s.tr[...] = jnp.transpose(s.fn[...])

    def up_chunk(g):
        for m in range(4):
            v = dot(s.tr[...], s.slope[m, :, 256 * g : 256 * g + 256])
            s.act[m, 0:D] = v.astype(BF)

    def put_chunk(slot, last=(3, 0)):
        @pl.loop(0, 16, unroll=4)
        def _(i):
            a, b, c = i // 8, lax.rem(i // 2, 4), lax.rem(i, 2)
            at = pl.multiple_of(48 * i, 16)
            parts = [s.act[m, pl.ds(at, 48)] for m in range(3)]
            v = jnp.concatenate(parts + [s.act[last[0], pl.ds(at + last[1], 48)]], axis=0)
            s.gr[slot, a, b, c] = dot(s.perm[...], v).astype(BF).reshape(4, 48, 256)

    up_chunk(0)
    put_chunk(3)
    rs("d3")

    @pl.loop(0, T // ROWS)
    def _(i):
        rows = pl.ds(pl.multiple_of(i * ROWS, ROWS), ROWS)
        u = s.acc[rows, :]
        n = s.n1[rows, :]
        r = s.rs1[rows, 0:1]
        ug = u * s.vec[3:4, :]
        grad = r * (ug - jnp.mean(ug, axis=1, keepdims=True) - n * jnp.mean(ug * n, axis=1, keepdims=True))
        low = grad.astype(BF)
        s.acc[rows, :] = grad
        s.gb[rows, :] = low
        fold(0, low.astype(F32))
        fold(1, u * n)
        fold(2, u)

    rs("20", "13")
    up_chunk(1)
    put_chunk(0)
    rs("d4", "21")
    up_chunk(2)
    put_chunk(1)
    rs("d5", "14")
    gav = s.gb[...]
    s.fn[...] = dot_nt(gav, weight_row(0, 3)).astype(BF)
    for i in range(6):
        s.vg[2 + i : 3 + i, :] = jnp.sum(s.vp[i], axis=0, keepdims=True)
    v_step(False, 0)
    s.tr[...] = jnp.transpose(s.ctx[...])
    out_at = ((3, 0), (3, D), (2, D))
    for g in range(3):
        m, at = out_at[g]
        s.act[m, at : at + D] = dot(s.tr[...], gav[:, 256 * g : 256 * g + 256]).astype(BF)
    s.tr[...] = jnp.transpose(s.x[...])
    s.lo[4] = jnp.zeros((8, 256), F32)
    rs("15", "22", "30")

    for g in range(3):
        @pl.loop(0, 2)
        def _(j):
            lanes = pl.ds(pl.multiple_of(j * 128, 128), 128)
            q = s.qkv[0, g, :, lanes]
            k = s.qkv[1, g, :, lanes]
            v = s.qkv[2, g, :, lanes]
            go = s.fn[:, pl.ds(pl.multiple_of(g * 256 + j * 128, 128), 128)]
            kt = jnp.transpose(k)
            gk = jnp.zeros((T, 128), F32)
            gvv = jnp.zeros((T, 128), F32)
            gqs = []
            for h in range(2):
                w = s.p[4 * g + 2 * j + h]
                wf = w.astype(F32)
                dw = dot_nt(head_only(v, h), go)
                ds = (wf * (dw - jnp.sum(wf * dw, axis=0, keepdims=True))).astype(BF)
                gqs.append(dot(kt[64 * h : 64 * h + 64], ds))
                gk = gk + dot(ds, head_only(q, h))
                gvv = gvv + dot(w, head_only(go, h))
            gq = (jnp.concatenate(gqs, axis=0) * 0.125).astype(BF)
            s.qkv[0, g, :, lanes] = jnp.transpose(gq)
            s.qkv[1, g, :, lanes] = (gk * 0.125).astype(BF)
            s.qkv[2, g, :, lanes] = gvv.astype(BF)

        rs(*EVENTS[g])
        v_step(False, 1 + g)
        if g == 0:
            pl.semaphore_wait(s.ready, len(partners))
        for m in range(3):
            s.act[m, 0:D] = dot(s.tr[...], s.qkv[m, g]).astype(BF)
        for i, m in ((g, 0), (3 + g, 2)):
            s.lo[4, i : i + 1, :] = jnp.sum(s.qkv[m, g].astype(F32), axis=0, keepdims=True)
        put_chunk((6 + g) % 4, out_at[g])
        rs("d%d" % (6 + g))

    v_step(True, 0)
    v_step(False, 4)
    @pl.loop(0, 3)
    def _(m):
        s.acc[...] += dot_nt(jnp.concatenate([s.qkv[m, g] for g in range(3)], axis=1), weight_row(0, m))

    s.o_ig[...] = s.acc[...].astype(BF)
    rs("18", "f4", "x3", "36", "27", "f5", "x4")
    v_step(True, 1)
    rs("28", "x5")
    v_step(True, 2)
    v_step(False, 5)
    rs("f6", "37")
    v_step(True, 3)
    rs("38", "f7", "x6")
    v_step(True, 4)
    rs("f8", "x7", "x8")

    s.vg[mine, :] = s.vo[3]
    s.vg[half, :] = s.vo[4]
    for g in range(3):
        s.vg[0:1, 256 * g : 256 * g + 256] = s.lo[3, g : g + 1, :]
        s.vg[1:2, 256 * g : 256 * g + 256] = s.lo[3, 3 + g : 4 + g, :]
    for g in range(3):
        lo = 256 * g
        v = s.fin[6 + g]
        for m in range(3):
            s.o_qkv[:, m * D + lo : m * D + lo + 256] = v[12 * m : 12 * m + 12]
        s.o_wout[:, lo : lo + 256] = v[36:48]
        v = s.fin[3 + g]
        for m in range(4):
            s.o_up[:, m * D + lo : m * D + lo + 256] = v[12 * m : 12 * m + 12]
        s.o_down[:, lo : lo + 256] = s.fin[g]
    vg = s.vg[...]
    lane_f = lax.broadcasted_iota(jnp.int32, (D, 128), 0)
    lane_r = lax.broadcasted_iota(jnp.int32, (D, 128), 1)
    pick = jnp.logical_and(lane_f - 12 * fs == lane_r, lane_r < 12).astype(F32)
    pick_up = jnp.logical_and(lane_f - 48 * lax.rem(fs, 16) == lane_r, lane_r < 48).astype(F32)
    exact = functools.partial(
        lax.dot_general, dimension_numbers=(((1,), (0,)), ((), ())), precision=lax.Precision.HIGHEST,
        preferred_element_type=F32,
    )
    thin = exact(vg, pick)
    thin_up = exact(vg, pick_up)
    quarter = fs // 16
    row_i = lax.broadcasted_iota(jnp.int32, (16, 128), 0)
    up_row = jnp.sum(jnp.where(row_i == 8 + quarter, thin_up, 0.0), axis=0, keepdims=True)
    s.o_vec[...] = jnp.where(row_i == 8, up_row, thin)


VECTORS = ((0, 12), (1, 12), (2, 12), (3, 12), (4, 12), (8, 48), (5, 12), (6, 12), (7, 12))


def finish(*refs):
    whole, vec, results, thin = refs[:6], refs[6], refs[7:13], refs[13:22]
    held, sems = refs[22:28], refs[28]
    ins = [pltpu.make_async_copy(a, b, sems.at[0, i]) for i, (a, b) in enumerate(zip(whole, held))]
    outs = [pltpu.make_async_copy(a, b, sems.at[1, i]) for i, (a, b) in enumerate(zip(held, results))]
    for c in ins:
        c.start()
    for (i, n), ref in zip(VECTORS, thin):
        ref[...] = vec[i : i + 1, 0:n]
    for a, b in zip(ins, outs):
        a.wait()
        b.start()
    for c in outs:
        c.wait()


def body(
    inputs, segment_ids, cotangent, qkv_weight, query_bias, value_bias, out_weight, out_bias, attn_gain,
    attn_shift, up_weight, up_bias, down_weight, down_bias, ffn_gain, ffn_shift,
):
    row = lambda v: v.reshape(1, -1)
    vmem = pl.BlockSpec(memory_space=pltpu.VMEM)
    hbm = pl.BlockSpec(memory_space=pl.ANY)
    whole = (
        jax.ShapeDtypeStruct((T, D), BF),
        jax.ShapeDtypeStruct((T, D), BF),
        jax.ShapeDtypeStruct((12, 3 * D), F32),
        jax.ShapeDtypeStruct((12, D), F32),
        jax.ShapeDtypeStruct((12, FF), F32),
        jax.ShapeDtypeStruct((48, D), F32),
    )
    outs = pl.pallas_call(
        kernel,
        out_shape=whole + (jax.ShapeDtypeStruct((16, 128), F32),),
        in_specs=[hbm if name.endswith("_hbm") else vmem for name in INS],
        out_specs=(vmem,) * len(OUTS),
        scratch_shapes=[v for _, v in SCRATCH]
        + [pltpu.SemaphoreType.DMA(v) for _, v in SEMS]
        + [pltpu.SemaphoreType.REGULAR],
        compiler_params=pltpu.CompilerParams(
            collective_id=0, has_side_effects=True, vmem_limit_bytes=63 * 2**20
        ),
    )(
        inputs.reshape(T, D), segment_ids, cotangent.reshape(T, D), qkv_weight, row(query_bias),
        row(value_bias), out_weight, row(out_bias), row(attn_gain), row(attn_shift), up_weight,
        row(up_bias), down_weight, row(down_bias), row(ffn_gain), row(ffn_shift),
    )
    r = pl.pallas_call(
        finish,
        out_shape=whole + tuple(jax.ShapeDtypeStruct((1, n), F32) for _, n in VECTORS),
        in_specs=[hbm] * 6 + [vmem],
        out_specs=(hbm,) * 6 + (vmem,) * 9,
        scratch_shapes=[pltpu.VMEM(a.shape, a.dtype) for a in whole] + [pltpu.SemaphoreType.DMA((2, 6))],
    )(*outs)
    v = [a.reshape(-1) for a in r[6:]]
    return (
        r[0].reshape(1, T, D), r[1].reshape(1, T, D), r[2], v[0], v[1], r[3], v[2], v[3], v[4], r[4], v[5],
        r[5], v[6], v[7], v[8],
    )


def solution(mesh):
    pages = P(("dp", "fsdp"), None, None)
    mat = P("fsdp", None)
    v = P("fsdp")
    in_specs = (pages, P(("dp", "fsdp"), None), pages, mat, v, v, mat, v, v, v, mat, v, mat, v, v, v)
    out_specs = (pages, pages, mat, v, v, mat, v, v, v, mat, v, mat, v, v, v)
    return jax.shard_map(body, mesh=mesh, in_specs=in_specs, out_specs=out_specs, check_vma=False)
```

```python
import functools
import types

import jax
import jax.numpy as jnp
from jax import lax
from jax.experimental import pallas as pl
from jax.experimental.pallas import tpu as pltpu
from jax.sharding import PartitionSpec as P

T = 512
D = 768
FF = 3072
BF = jnp.bfloat16
F32 = jnp.float32
MESH = pl.DeviceIdType.MESH
ROWS = 128
BLOCK = (2, 4, 2, 4, 48, 256)

SCRATCH = (
    ("G", pltpu.VMEM((9,) + BLOCK, BF)),
    ("GV", pltpu.VMEM((2, 4, 2, 4, 16, 128), BF)),
    ("gr", pltpu.VMEM((4,) + BLOCK, BF)),
    ("rd", pltpu.VMEM((6, 4, 2, 4, 48, 256), BF)),
    ("r1", pltpu.VMEM((6, 3, 4, 2, 48, 256), BF)),
    ("r2", pltpu.VMEM((6, 7, 2, 48, 256), BF)),
    ("r3", pltpu.VMEM((6, 4, 48, 256), BF)),
    ("fin", pltpu.VMEM((9, 48, 256), F32)),
    ("qkv", pltpu.VMEM((3, 3, T, 256), BF)),
    ("p", pltpu.VMEM((12, T, T), BF)),
    ("mask", pltpu.VMEM((T, T), BF)),
    ("ctx", pltpu.VMEM((T, D), BF)),
    ("n1", pltpu.VMEM((T, D), F32)),
    ("rs1", pltpu.VMEM((T, 128), F32)),
    ("fn", pltpu.VMEM((T, D), BF)),
    ("act", pltpu.VMEM((4, 3 * T, 256), BF)),
    ("slope", pltpu.VMEM((4, T, D), BF)),
    ("acc", pltpu.VMEM((T, D), F32)),
    ("gb", pltpu.VMEM((T, D), BF)),
    ("tr", pltpu.VMEM((D, T), BF)),
    ("perm", pltpu.VMEM((192, 192), BF)),
    ("vec", pltpu.VMEM((16, D), F32)),
    ("ub", pltpu.VMEM((8, FF), F32)),
    ("vg", pltpu.VMEM((16, D), F32)),
    ("va", pltpu.VMEM((14, 8, D), F32)),
    ("vo", pltpu.VMEM((5, 8, D), F32)),
    ("la", pltpu.VMEM((14, 8, 256), F32)),
    ("lo", pltpu.VMEM((5, 8, 256), F32)),
    ("vp", pltpu.VMEM((6, 8, D), F32)),
    ("small", pltpu.VMEM((16, 128), F32)),
    ("x", pltpu.VMEM((T, D), BF)),
    ("ct", pltpu.VMEM((T, D), BF)),
    ("own", pltpu.VMEM((48, 256), F32)),
)
SEMS = (
    ("zs", (10, 7)), ("zr", (10, 4)), ("xs", (10, 3)), ("xr", (10, 3)),
    ("ys", (10, 2)), ("yr", (10, 2)), ("ds", (10,)), ("dr", (10,)),
    ("rds", (9,)), ("rdr", (9,)), ("p1s", (9, 3)), ("p1r", (9, 3)),
    ("p2s", (9, 4)), ("p2r", (9, 7)), ("p3s", (9, 4)), ("p3r", (9, 4)),
    ("fs", (9,)), ("fr", (9,)), ("vs", (30,)), ("vr", (30,)), ("ls", (2,)),
)
INS = (
    "x_hbm", "seg", "ct_hbm", "wqkv", "qb", "vb", "wout", "ob", "ag", "ash",
    "wup", "ub_in", "wdown", "db", "fg", "fsh",
)
OUTS = ("o_out", "o_ig", "o_qkv", "o_wout", "o_up", "o_down", "o_vec")


EVENTS = (
    ("31", "f0", "23", "32"),
    ("24", "33", "16", "f1", "x0", "f2", "25"),
    ("34", "17", "f3", "35", "x1", "x2", "26"),
)


def dot(a, b):
    return lax.dot_general(a, b, (((1,), (0,)), ((), ())), preferred_element_type=F32)


def dot_nt(a, b):
    return lax.dot_general(a, b, (((1,), (1,)), ((), ())), preferred_element_type=F32)


def device(x, y, z, c):
    return ((y // 2) * 2 + c, z * 8 + lax.rem(y, 2) * 4 + x)


def kernel(*refs):
    names = INS + OUTS + tuple(n for n, _ in SCRATCH) + tuple(n for n, _ in SEMS) + ("ready",)
    s = types.SimpleNamespace(**dict(zip(names, refs, strict=True)))
    dp, fs = lax.axis_index("dp"), lax.axis_index("fsdp")
    C = lax.rem(dp, 2)
    YH = dp // 2
    Z = fs // 8
    YL = lax.rem(fs // 4, 2)
    X = lax.rem(fs, 4)
    Y = YH * 2 + YL
    ZT = Z // 4
    ZL = lax.rem(Z, 4)

    def copy(src, dst, send, recv, where):
        return pltpu.make_async_remote_copy(
            src_ref=src, dst_ref=dst, send_sem=send, recv_sem=recv, device_id=where, device_id_type=MESH
        )

    sibling = device(X, Y, Z, 1 - C)
    partners = (
        [sibling]
        + [device(lax.rem(X + d, 4), Y, Z, C) for d in (1, 2, 3)]
        + [device(X, lax.rem(Y + d, 4), Z, C) for d in (1, 2, 3)]
        + [device(X, Y, lax.rem(Z + d, 8), C) for d in range(1, 8)]
        + [device(lax.rem(X + d, 4), lax.rem(Y + 2, 4), Z, C) for d in (1, 2, 3)]
    )

    def greet(sem):
        for where in partners:
            pl.semaphore_signal(sem, inc=1, device_id=where, device_id_type=MESH)

    def gref(k):
        return s.GV if isinstance(k, int) and k == 9 else s.G.at[k]

    def z_copy(k, d):
        here = gref(k).at[ZT, ZL, YL, X]
        return copy(here, here, s.zs.at[k, d - 1], s.zr.at[k, ZL], device(X, Y, lax.rem(Z + d, 8), C))

    def z_recv(k, zl):
        here = gref(k).at[C, zl, YL, X]
        return copy(here, here, s.zs.at[k, 0], s.zr.at[k, zl], sibling)

    def x_copy(k, d):
        here = gref(k).at[C, :, YL, X]
        return copy(here, here, s.xs.at[k, d - 1], s.xr.at[k, d - 1], device(lax.rem(X + d, 4), Y, Z, C))

    def y_copy(k, i):
        here = gref(k).at[C, :, YL, pl.ds(2 * i, 2)]
        return copy(here, here, s.ys.at[k, i], s.yr.at[k, i], device(X, lax.rem(Y + 1 + 2 * i, 4), Z, C))

    def d_copy(k):
        here = gref(k).at[C]
        return copy(here, here, s.ds.at[k], s.dr.at[k], sibling)

    def last_x(d):
        here = s.G.at[8, ZT, ZL, YL, X]
        return copy(here, here, s.xs.at[8, d - 1], s.xr.at[8, d - 1], device(lax.rem(X + d, 4), Y, Z, C))

    def last_y(i):
        here = s.G.at[8, ZT, ZL, YL, pl.ds(2 * i, 2)]
        return copy(here, here, s.ys.at[8, i], s.yr.at[8, i], device(X, lax.rem(Y + 1 + 2 * i, 4), Z, C))

    def last_z(d):
        here = s.G.at[8, ZT, ZL]
        return copy(here, here, s.zs.at[8, d - 1], s.zr.at[8, ZL], device(X, Y, lax.rem(Z + d, 8), C))

    def last_got(zl):
        here = s.G.at[8, C, zl]
        return copy(here, here, s.zs.at[8, 0], s.zr.at[8, zl], sibling)

    def last_step(n):
        @pl.when(C == ZT)
        def _():
            if n == 0:
                for d in (2, 1, 3):
                    last_x(d).start()
            elif n == 1:
                for d in (1, 2, 3):
                    last_x(d).wait()
                for i in (0, 1):
                    last_y(i).start()
            elif n == 2:
                for i in (0, 1):
                    last_y(i).wait()
                for d in (4, 3, 5, 2, 6, 1, 7):
                    last_z(d).start()
            elif n == 4:
                for d in range(1, 8):
                    last_z(d).wait_send()

        if n == 3:
            for zl in range(4):
                @pl.when(jnp.logical_or(C != ZT, zl != ZL))
                def _():
                    last_got(zl).wait_recv()
            d_copy(8).start()
        elif n == 4:
            d_copy(8).wait()

    def ag_x(k):
        for zl in range(4):
            @pl.when(jnp.logical_or(C != ZT, zl != ZL))
            def _():
                z_recv(k, zl).wait_recv()
        for d in (2, 1, 3):
            x_copy(k, d).start()

    def ag_y(k):
        for d in (1, 2, 3):
            x_copy(k, d).wait_recv()
        for i in (0, 1):
            y_copy(k, i).start()

    def ag_d(k):
        for i in (0, 1):
            y_copy(k, i).wait_recv()
        d_copy(k).start()

    def ag_done(k):
        d_copy(k).wait()
        @pl.when(C == ZT)
        def _():
            for d in range(1, 8):
                z_copy(k, d).wait_send()
        for d in (1, 2, 3):
            x_copy(k, d).wait_send()
        for i in (0, 1):
            y_copy(k, i).wait_send()

    sends = {"x": ag_x, "y": ag_y, "d": ag_d, "l": last_step}

    def ag(*events):
        for e in events:
            sends[e[0]](int(e[1]))

    barrier = pltpu.get_barrier_semaphore()
    greet(barrier)
    load_x = pltpu.make_async_copy(s.x_hbm, s.x, s.ls.at[0])
    load_x.start()
    load_ct = pltpu.make_async_copy(s.ct_hbm, s.ct, s.ls.at[1])
    load_ct.start()

    def own_block(k, parts):
        for m, part in enumerate(parts):
            s.own[12 * m : 12 * m + 12, :] = part.astype(F32)
        s.G[k, ZT, ZL, YL, X] = s.own[...].astype(BF)

    def pack(k):
        lo = 256 * (k % 3)
        if k < 3:
            own_block(k, [s.wqkv[:, m * D + lo : m * D + lo + 256] for m in range(3)] + [s.wout[:, lo : lo + 256]])
        elif k < 6:
            own_block(k, [s.wup[:, m * D + lo : m * D + lo + 256] for m in range(4)])
        else:
            s.G[k, ZT, ZL, YL, X] = s.wdown[:, lo : lo + 256]

    @pl.when(C == ZT)
    def _():
        pack(0)
        s.small[...] = jnp.zeros((16, 128), F32)
        for i, v in enumerate((s.qb, s.vb, s.ob, s.ag, s.ash, s.db, s.fg, s.fsh)):
            s.small[i : i + 1, 0:12] = v[...].astype(F32)
        s.small[8:9, 0:48] = s.ub_in[...].astype(F32)
        s.GV[ZT, ZL, YL, X] = s.small[...].astype(BF)

    pl.semaphore_wait(barrier, len(partners))

    @pl.when(C == ZT)
    def _():
        for k in (9, 0, 1, 2, 3, 4, 5, 6, 7, 8):
            if 1 <= k <= 8:
                pack(k)
            if k < 8 or k == 9:
                for d in (4, 3, 5, 2, 6, 1, 7):
                    z_copy(k, d).start()

    row = lax.broadcasted_iota(jnp.int32, (192, 192), 0)
    col = lax.broadcasted_iota(jnp.int32, (192, 192), 1)
    swapped = lax.rem(row // 12, 4) * 48 + (row // 48) * 12 + lax.rem(row, 12)
    s.perm[...] = (col == swapped).astype(F32).astype(BF)
    segf = jnp.broadcast_to(s.seg[...].astype(F32), (128, T))
    seg_col = jnp.transpose(segf)[:, 0:1]
    s.mask[...] = jnp.where(seg_col == segf[0:1, :], 0.0, -1e30).astype(BF)
    s.vg[...] = jnp.zeros((16, D), F32)
    s.vp[...] = jnp.zeros((6, 8, D), F32)

    def reorder(src, dst):
        @pl.loop(0, 16, unroll=4)
        def _(i):
            a, b, c = i // 8, lax.rem(i // 2, 4), lax.rem(i, 2)
            v = src[a, b, c].reshape(192, 256)
            w = dot(s.perm[...], v).astype(BF)
            dst[a, b, c] = w.reshape(4, 48, 256)

    def weight(k, m):
        return s.G[k, :, :, :, m].reshape(D, 256)

    def weight_row(base, m):
        return jnp.concatenate([weight(base + g, m) for g in range(3)], axis=1)

    def down_rows(m):
        parts = [s.G[6 + g, m // 2, pl.ds(2 * (m % 2), 2)].reshape(D, 256) for g in range(3)]
        return jnp.concatenate(parts, axis=1)

    def active(m):
        return jnp.concatenate([s.act[m, T * g : T * g + T] for g in range(3)], axis=1)

    ag("l0", "x9", "x0", "y9", "x1", "d9", "x2", "l1", "y0")
    ag_done(9)
    load_x.wait()
    load_ct.wait()

    pick_r = lax.broadcasted_iota(jnp.int32, (128, D), 0)
    pick_c = lax.broadcasted_iota(jnp.int32, (128, D), 1)
    s.vec[...] = jnp.zeros((16, D), F32)
    s.ub[...] = jnp.zeros((8, FF), F32)

    @pl.loop(0, 8, unroll=2)
    def _(i):
        gv = s.GV[i // 4, lax.rem(i, 4)].reshape(128, 128)
        wide = dot(gv, (lax.rem(pick_c, 12) == pick_r).astype(F32).astype(BF))
        owner = lax.broadcasted_iota(jnp.int32, (128, D), 0) // 16 + 8 * i
        lane = lax.broadcasted_iota(jnp.int32, (128, D), 1) // 12
        s.vec[...] += jnp.sum(jnp.where(owner == lane, wide, 0.0).reshape(8, 16, D), axis=0)
        sel_r = lax.broadcasted_iota(jnp.int32, (8, 128), 0)
        sel_c = lax.broadcasted_iota(jnp.int32, (8, 128), 1)
        rows8 = dot((sel_c == 16 * sel_r + 8).astype(F32).astype(BF), gv).astype(BF)
        for m in range(4):
            up_c = pick_c + m * D
            wide_up = dot(rows8, (lax.rem(up_c, 48) == pick_r).astype(F32).astype(BF))
            own_r = lax.broadcasted_iota(jnp.int32, (8, D), 0) + 8 * i
            own_c = (lax.broadcasted_iota(jnp.int32, (8, D), 1) + m * D) // 48
            s.ub[:, m * D : m * D + D] += jnp.where(own_r == own_c, wide_up, 0.0)

    s.ub[0:1, :] = jnp.sum(s.ub[...], axis=0, keepdims=True)

    ag("x3", "y1", "x4", "x5", "l2", "d0", "y2")

    head_lane = lax.broadcasted_iota(jnp.int32, (1, 128), 1) // 64

    def head_only(v, h):
        return jnp.where(head_lane == h, v, jnp.zeros_like(v))

    for g in range(3):
        ag_done(g)
        reorder(s.G.at[g], s.G.at[g])
        xv = s.x[...]
        for m in range(3):
            v = dot(xv, weight(g, m))
            if m != 1:
                i = 0 if m == 0 else 1
                v = v + s.vec[i : i + 1, 256 * g : 256 * g + 256]
            s.qkv[m, g] = v.astype(BF)
        ag(*(("d1", "y3", "x6", "x7"), ("d3",), ("y6",))[g])

        @pl.loop(0, 2)
        def _(j):
            lanes = pl.ds(pl.multiple_of(j * 128, 128), 128)
            q = s.qkv[0, g, :, lanes] * 0.125
            k = s.qkv[1, g, :, lanes]
            v = s.qkv[2, g, :, lanes]
            vt = jnp.transpose(v)
            outs = []
            for h in range(2):
                sc = dot_nt(head_only(k, h), q) + s.mask[...].astype(F32)
                e = jnp.exp(sc - jnp.max(sc, axis=0, keepdims=True))
                w = (e * (1.0 / jnp.sum(e, axis=0, keepdims=True))).astype(BF)
                s.p[4 * g + 2 * j + h] = w
                outs.append(dot(vt[64 * h : 64 * h + 64], w))
            out = jnp.transpose(jnp.concatenate(outs, axis=0).astype(BF))
            s.ctx[:, pl.ds(pl.multiple_of(g * 256 + j * 128, 128), 128)] = out

        ag(*(("d2", "y4"), ("y5", "d4"), ("d5", "y7"))[g])

    cv = s.ctx[...]
    for g in range(3):
        s.acc[:, 256 * g : 256 * g + 256] = dot(cv, weight(g, 3))

    @pl.loop(0, T // ROWS)
    def _(i):
        rows = pl.ds(pl.multiple_of(i * ROWS, ROWS), ROWS)
        v = s.acc[rows, :] + s.vec[2:3, :] + s.x[rows, :].astype(F32)
        v = v - jnp.mean(v, axis=1, keepdims=True)
        r = lax.rsqrt(jnp.mean(v * v, axis=1, keepdims=True) + 1e-12)
        n = v * r
        s.n1[rows, :] = n
        s.rs1[rows, :] = jnp.broadcast_to(r, (ROWS, 128))
        s.fn[rows, :] = (n * s.vec[3:4, :] + s.vec[4:5, :]).astype(BF)

    fv = s.fn[...]
    ag("d6")
    for g in range(3):
        if g == 1:
            ag("d7", "l3")
        ag_done(3 + g)
        reorder(s.G.at[3 + g], s.G.at[3 + g])
        for m in range(4):
            lo = 256 * g
            u = dot(fv, weight(3 + g, m)) + s.ub[0:1, m * D + lo : m * D + lo + 256]
            half = 0.5 * (1.0 + lax.erf(u * 0.7071067811865476))
            s.act[m, T * g : T * g + T] = (u * half).astype(BF)
            s.slope[m, :, lo : lo + 256] = (half + u * jnp.exp(-0.5 * u * u) * 0.3989422804014327).astype(BF)
    for g in range(3):
        if g < 2:
            ag_done(6 + g)
        else:
            last_step(4)
        lo = 256 * g
        total = jnp.zeros((T, 256), F32)
        for m in range(4):
            total = total + dot(active(m), s.G[6 + g, m // 2, 2 * (m % 2) : 2 * (m % 2) + 2].reshape(D, 256))
        s.acc[:, lo : lo + 256] = total

    def fold(i, v):
        s.vp[i] += jnp.sum(v.reshape(ROWS // 8, 8, D), axis=0)

    @pl.loop(0, T // ROWS)
    def _(i):
        rows = pl.ds(pl.multiple_of(i * ROWS, ROWS), ROWS)
        v = s.acc[rows, :] + s.vec[5:6, :] + s.fn[rows, :].astype(F32)
        v = v - jnp.mean(v, axis=1, keepdims=True)
        r = lax.rsqrt(jnp.mean(v * v, axis=1, keepdims=True) + 1e-12)
        n = v * r
        gain = s.vec[6:7, :]
        s.o_out[rows, :] = (n * gain + s.vec[7:8, :]).astype(BF)
        u = s.ct[rows, :].astype(F32)
        ug = u * gain
        un = u * n
        grad = r * (ug - jnp.mean(ug, axis=1, keepdims=True) - n * jnp.mean(ug * n, axis=1, keepdims=True))
        low = grad.astype(BF)
        s.acc[rows, :] = grad
        s.gb[rows, :] = low
        fold(3, low.astype(F32))
        fold(4, un)
        fold(5, u)

    def rd(j):
        return s.rd.at[j] if j < 6 else s.G.at[j, 0]

    def r1(j, d):
        return s.r1.at[j, d] if j < 6 else s.G.at[j, 1, :, :, d]

    def r2(j, slot):
        return s.r2.at[j, slot] if j < 6 else s.G.at[j - 3, slot // 4, lax.rem(slot, 4), :, 0]

    def r3(j, slot):
        return s.r3.at[j, slot] if j < 6 else s.G.at[j - 3, 0, slot, 0, 1]

    def rd_copy(j):
        return copy(
            s.gr.at[j % 4, 1 - C], rd(j), s.rds.at[j], s.rdr.at[j], sibling
        )

    def p1_copy(j, d, c):
        if c == 0:
            xx = lax.rem(X + d, 4)
            src, where = s.gr.at[j % 4, 0, :, :, xx], device(xx, Y, Z, 0)
        else:
            yy = lax.rem(Y + d, 4)
            src = s.gr.at[j % 4, 1, :, lax.rem(yy, 2), pl.ds(2 * (yy // 2), 2)]
            where = device(X, yy, Z, 1)
        return copy(src, r1(j, d - 1), s.p1s.at[j, d - 1], s.p1r.at[j, d - 1], where)

    def p2_copy(j, zl):
        zz = C * 4 + zl
        slot = lax.rem(Z - zz + 8, 8) - 1
        return copy(
            r1(j, 0).at[zl], r2(j, slot), s.p2s.at[j, zl], s.p2r.at[j, slot],
            device(X, Y, zz, C),
        )

    def p2_recv(j, slot):
        return copy(
            r1(j, 0).at[0], r2(j, slot), s.p2s.at[j, 0], s.p2r.at[j, slot], sibling
        )

    def p3_copy0(j, d):
        yy = lax.rem(Y + d, 4)
        return copy(
            r2(j, 0).at[lax.rem(yy, 2)], r3(j, Y), s.p3s.at[j, d], s.p3r.at[j, Y],
            device(X, yy, Z, 0),
        )

    def p3_copy1(j, i, other):
        xx = 2 * YH + i
        yy = lax.rem(Y + 2 * other, 4)
        return copy(
            r2(j, 0).at[i], r3(j, X), s.p3s.at[j, 2 * i + other], s.p3r.at[j, X],
            device(xx, yy, Z, 1),
        )

    def p3_recv(j, slot):
        return copy(
            r2(j, 0).at[0], r3(j, slot), s.p3s.at[j, 0], s.p3r.at[j, slot], sibling
        )

    def f_copy(j):
        here = s.fin.at[j]
        return copy(here, here, s.fs.at[j], s.fr.at[j], sibling)

    def rs_d(j):
        rd_copy(j).start()

    def rs_p1(j):
        rd_copy(j).wait()

        @pl.loop(0, 8, unroll=2)
        def _(i):
            a, b = i // 2, lax.rem(i, 2)
            v = s.gr[j % 4, C, a, b].astype(F32) + rd(j)[a, b].astype(F32)
            s.gr[j % 4, C, a, b] = v.astype(BF)

        for c in (0, 1):
            @pl.when(C == c)
            def _():
                for d in (2, 1, 3):
                    p1_copy(j, d, c).start()

    def rs_p2(j):
        for c in (0, 1):
            @pl.when(C == c)
            def _():
                for d in (1, 2, 3):
                    p1_copy(j, d, c).wait()

        @pl.loop(0, 8, unroll=2)
        def _(i):
            a, b = i // 2, lax.rem(i, 2)
            mine = s.gr[j % 4, C, a, jnp.where(C == 0, b, YL), jnp.where(C == 0, X, 2 * YH + b)]
            v = mine.astype(F32)
            for d in range(3):
                v = v + r1(j, d)[a, b].astype(F32)
            r1(j, 0)[a, b] = v.astype(BF)

        for zl in range(4):
            @pl.when(C * 4 + zl != Z)
            def _():
                p2_copy(j, zl).start()

    def rs_p3(j):
        @pl.when(C == ZT)
        def _():
            for slot in range(7):
                p2_recv(j, slot).wait_recv()
            for b in range(2):
                v = r1(j, 0)[ZL, b].astype(F32)
                for slot in range(7):
                    v = v + r2(j, slot)[b].astype(F32)
                r2(j, 0)[b] = v.astype(BF)

        @pl.when(jnp.logical_and(C == 0, ZT == 0))
        def _():
            for d in (1, 2, 3):
                p3_copy0(j, d).start()

        @pl.when(jnp.logical_and(C == 1, ZT == 1))
        def _():
            for i in range(2):
                p3_copy1(j, i, 1).start()

                @pl.when(X != 2 * YH + i)
                def _():
                    p3_copy1(j, i, 0).start()

    def rs_f(j):
        own_slot = jnp.where(C == 0, Y, X)
        has_own = jnp.logical_or(C == 0, YH == X // 2)

        @pl.when(C == ZT)
        def _():
            @pl.when(has_own)
            def _():
                r3(j, own_slot)[...] = r2(j, 0)[jnp.where(C == 0, YL, lax.rem(X, 2))]
            for slot in range(4):
                @pl.when(jnp.logical_not(jnp.logical_and(has_own, own_slot == slot)))
                def _():
                    p3_recv(j, slot).wait_recv()
            v = r3(j, 0)[...].astype(F32)
            for slot in range(1, 4):
                v = v + r3(j, slot)[...].astype(F32)
            s.fin[j] = v
            f_copy(j).start()

    def rs_done(j):
        for zl in range(4):
            @pl.when(C * 4 + zl != Z)
            def _():
                p2_copy(j, zl).wait_send()

        @pl.when(jnp.logical_and(C == 0, ZT == 0))
        def _():
            for d in (1, 2, 3):
                p3_copy0(j, d).wait_send()

        @pl.when(jnp.logical_and(C == 1, ZT == 1))
        def _():
            for i in range(2):
                p3_copy1(j, i, 1).wait_send()

                @pl.when(X != 2 * YH + i)
                def _():
                    p3_copy1(j, i, 0).wait_send()

        @pl.when(C == ZT)
        def _():
            f_copy(j).wait_send()

        @pl.when(C != ZT)
        def _():
            f_copy(j).wait_recv()

    stages = {"d": rs_d, "1": rs_p1, "2": rs_p2, "3": rs_p3, "f": rs_f, "x": rs_done}

    def rs(*events):
        for e in events:
            stages[e[0]](int(e[1]))

    half = pl.ds(pl.multiple_of((1 - C) * 8, 8), 8)
    mine = pl.ds(pl.multiple_of(C * 8, 8), 8)
    axes = (
        [device(X, Y, lax.rem(Z + d, 8), C) for d in range(1, 8)],
        [device(lax.rem(X + d, 4), Y, Z, C) for d in (1, 2, 3)],
        [device(X, lax.rem(Y + d, 4), Z, C) for d in (1, 2, 3)],
    )
    starts = (1, 8, 11)

    def v_moves(late, step):
        held, got = (s.lo, s.la) if late else (s.vo, s.va)
        base = 15 if late else 0

        def move(src, dst, i, where):
            return copy(src, dst, s.vs.at[base + i], s.vr.at[base + i], where)

        if step == 0:
            return [move(held.at[4] if late else s.vg.at[half], got.at[0], 0, sibling)]
        if step == 4:
            return [move(held.at[3], held.at[4], 14, sibling)]
        first = starts[step - 1]
        return [move(held.at[step - 1], got.at[first + i], first + i, where) for i, where in enumerate(axes[step - 1])]

    def v_step(late, step):
        held, got = (s.lo, s.la) if late else (s.vo, s.va)
        if step:
            for c in v_moves(late, step - 1):
                c.wait()
        if step == 1:
            held[0] = (held[4] if late else s.vg[mine, :]) + got[0]
        elif 2 <= step <= 4:
            first = starts[step - 2]
            v = held[step - 2]
            for i in range(len(axes[step - 2])):
                v = v + got[first + i]
            held[step - 1] = v
        if step < (4 if late else 5):
            for c in v_moves(late, step):
                c.start()

    gbv = s.gb[...]
    for m in range(4):
        s.tr[...] = jnp.transpose(active(m))
        for g in range(3):
            v = dot(s.tr[...], gbv[:, 256 * g : 256 * g + 256])
            s.gr[g, m // 2, 2 * (m % 2) : 2 * (m % 2) + 2] = v.astype(BF).reshape(2, 2, 4, 48, 256)
    rs("d0", "d1", "d2")
    for m in range(4):
        low = (dot_nt(gbv, down_rows(m)) * s.slope[m].astype(F32)).astype(BF)
        s.slope[m] = low
        s.vg[8 + m : 9 + m, :] = jnp.sum(low.astype(F32), axis=0, keepdims=True)
    rs("10", "11", "12")
    @pl.loop(0, 4)
    def _(m):
        s.acc[...] += dot_nt(s.slope[m], weight_row(3, m))

    greet(s.ready)
    s.tr[...] = jnp.transpose(s.fn[...])

    def up_chunk(g):
        for m in range(4):
            v = dot(s.tr[...], s.slope[m, :, 256 * g : 256 * g + 256])
            s.act[m, 0:D] = v.astype(BF)

    def put_chunk(slot, last=(3, 0)):
        @pl.loop(0, 16, unroll=4)
        def _(i):
            a, b, c = i // 8, lax.rem(i // 2, 4), lax.rem(i, 2)
            at = pl.multiple_of(48 * i, 16)
            parts = [s.act[m, pl.ds(at, 48)] for m in range(3)]
            v = jnp.concatenate(parts + [s.act[last[0], pl.ds(at + last[1], 48)]], axis=0)
            s.gr[slot, a, b, c] = dot(s.perm[...], v).astype(BF).reshape(4, 48, 256)

    up_chunk(0)
    put_chunk(3)
    rs("d3")

    @pl.loop(0, T // ROWS)
    def _(i):
        rows = pl.ds(pl.multiple_of(i * ROWS, ROWS), ROWS)
        u = s.acc[rows, :]
        n = s.n1[rows, :]
        r = s.rs1[rows, 0:1]
        ug = u * s.vec[3:4, :]
        grad = r * (ug - jnp.mean(ug, axis=1, keepdims=True) - n * jnp.mean(ug * n, axis=1, keepdims=True))
        low = grad.astype(BF)
        s.acc[rows, :] = grad
        s.gb[rows, :] = low
        fold(0, low.astype(F32))
        fold(1, u * n)
        fold(2, u)

    rs("20", "13")
    up_chunk(1)
    put_chunk(0)
    rs("d4", "21")
    up_chunk(2)
    put_chunk(1)
    rs("d5", "14")
    gav = s.gb[...]
    s.fn[...] = dot_nt(gav, weight_row(0, 3)).astype(BF)
    for i in range(6):
        s.vg[2 + i : 3 + i, :] = jnp.sum(s.vp[i], axis=0, keepdims=True)
    v_step(False, 0)
    s.tr[...] = jnp.transpose(s.ctx[...])
    out_at = ((3, 0), (3, D), (2, D))
    for g in range(3):
        m, at = out_at[g]
        s.act[m, at : at + D] = dot(s.tr[...], gav[:, 256 * g : 256 * g + 256]).astype(BF)
    s.tr[...] = jnp.transpose(s.x[...])
    s.lo[4] = jnp.zeros((8, 256), F32)
    rs("15", "22", "30")

    for g in range(3):
        @pl.loop(0, 2)
        def _(j):
            lanes = pl.ds(pl.multiple_of(j * 128, 128), 128)
            q = s.qkv[0, g, :, lanes]
            k = s.qkv[1, g, :, lanes]
            v = s.qkv[2, g, :, lanes]
            go = s.fn[:, pl.ds(pl.multiple_of(g * 256 + j * 128, 128), 128)]
            kt = jnp.transpose(k)
            gk = jnp.zeros((T, 128), F32)
            gvv = jnp.zeros((T, 128), F32)
            gqs = []
            for h in range(2):
                w = s.p[4 * g + 2 * j + h]
                wf = w.astype(F32)
                dw = dot_nt(head_only(v, h), go)
                ds = (wf * (dw - jnp.sum(wf * dw, axis=0, keepdims=True))).astype(BF)
                gqs.append(dot(kt[64 * h : 64 * h + 64], ds))
                gk = gk + dot(ds, head_only(q, h))
                gvv = gvv + dot(w, head_only(go, h))
            gq = (jnp.concatenate(gqs, axis=0) * 0.125).astype(BF)
            s.qkv[0, g, :, lanes] = jnp.transpose(gq)
            s.qkv[1, g, :, lanes] = (gk * 0.125).astype(BF)
            s.qkv[2, g, :, lanes] = gvv.astype(BF)

        rs(*EVENTS[g])
        v_step(False, 1 + g)
        if g == 0:
            pl.semaphore_wait(s.ready, len(partners))
        for m in range(3):
            s.act[m, 0:D] = dot(s.tr[...], s.qkv[m, g]).astype(BF)
        for i, m in ((g, 0), (3 + g, 2)):
            s.lo[4, i : i + 1, :] = jnp.sum(s.qkv[m, g].astype(F32), axis=0, keepdims=True)
        put_chunk((6 + g) % 4, out_at[g])
        rs("d%d" % (6 + g))

    v_step(True, 0)
    v_step(False, 4)
    @pl.loop(0, 3)
    def _(m):
        s.acc[...] += dot_nt(jnp.concatenate([s.qkv[m, g] for g in range(3)], axis=1), weight_row(0, m))

    s.o_ig[...] = s.acc[...].astype(BF)
    rs("18", "f4", "x3", "36", "27", "f5", "x4")
    v_step(True, 1)
    rs("28", "x5")
    v_step(True, 2)
    v_step(False, 5)
    rs("f6", "37")
    v_step(True, 3)
    rs("38", "f7", "x6")
    v_step(True, 4)
    rs("f8", "x7", "x8")

    s.vg[mine, :] = s.vo[3]
    s.vg[half, :] = s.vo[4]
    for g in range(3):
        s.vg[0:1, 256 * g : 256 * g + 256] = s.lo[3, g : g + 1, :]
        s.vg[1:2, 256 * g : 256 * g + 256] = s.lo[3, 3 + g : 4 + g, :]
    for g in range(3):
        lo = 256 * g
        v = s.fin[6 + g]
        for m in range(3):
            s.o_qkv[:, m * D + lo : m * D + lo + 256] = v[12 * m : 12 * m + 12]
        s.o_wout[:, lo : lo + 256] = v[36:48]
        v = s.fin[3 + g]
        for m in range(4):
            s.o_up[:, m * D + lo : m * D + lo + 256] = v[12 * m : 12 * m + 12]
        s.o_down[:, lo : lo + 256] = s.fin[g]
    vg = s.vg[...]
    lane_f = lax.broadcasted_iota(jnp.int32, (D, 128), 0)
    lane_r = lax.broadcasted_iota(jnp.int32, (D, 128), 1)
    pick = jnp.logical_and(lane_f - 12 * fs == lane_r, lane_r < 12).astype(F32)
    pick_up = jnp.logical_and(lane_f - 48 * lax.rem(fs, 16) == lane_r, lane_r < 48).astype(F32)
    exact = functools.partial(
        lax.dot_general, dimension_numbers=(((1,), (0,)), ((), ())), precision=lax.Precision.HIGHEST,
        preferred_element_type=F32,
    )
    thin = exact(vg, pick)
    thin_up = exact(vg, pick_up)
    quarter = fs // 16
    row_i = lax.broadcasted_iota(jnp.int32, (16, 128), 0)
    up_row = jnp.sum(jnp.where(row_i == 8 + quarter, thin_up, 0.0), axis=0, keepdims=True)
    s.o_vec[...] = jnp.where(row_i == 8, up_row, thin)


VECTORS = ((0, 12), (1, 12), (2, 12), (3, 12), (4, 12), (8, 48), (5, 12), (6, 12), (7, 12))


def finish(*refs):
    whole, vec, results, thin = refs[:6], refs[6], refs[7:13], refs[13:22]
    held, sems = refs[22:28], refs[28]
    ins = [pltpu.make_async_copy(a, b, sems.at[0, i]) for i, (a, b) in enumerate(zip(whole, held))]
    outs = [pltpu.make_async_copy(a, b, sems.at[1, i]) for i, (a, b) in enumerate(zip(held, results))]
    for c in ins:
        c.start()
    for (i, n), ref in zip(VECTORS, thin):
        ref[...] = vec[i : i + 1, 0:n]
    for a, b in zip(ins, outs):
        a.wait()
        b.start()
    for c in outs:
        c.wait()


def body(
    inputs, segment_ids, cotangent, qkv_weight, query_bias, value_bias, out_weight, out_bias, attn_gain,
    attn_shift, up_weight, up_bias, down_weight, down_bias, ffn_gain, ffn_shift,
):
    row = lambda v: v.reshape(1, -1)
    vmem = pl.BlockSpec(memory_space=pltpu.VMEM)
    hbm = pl.BlockSpec(memory_space=pl.ANY)
    whole = (
        jax.ShapeDtypeStruct((T, D), BF),
        jax.ShapeDtypeStruct((T, D), BF),
        jax.ShapeDtypeStruct((12, 3 * D), F32),
        jax.ShapeDtypeStruct((12, D), F32),
        jax.ShapeDtypeStruct((12, FF), F32),
        jax.ShapeDtypeStruct((48, D), F32),
    )
    outs = pl.pallas_call(
        kernel,
        out_shape=whole + (jax.ShapeDtypeStruct((16, 128), F32),),
        in_specs=[hbm if name.endswith("_hbm") else vmem for name in INS],
        out_specs=(vmem,) * len(OUTS),
        scratch_shapes=[v for _, v in SCRATCH]
        + [pltpu.SemaphoreType.DMA(v) for _, v in SEMS]
        + [pltpu.SemaphoreType.REGULAR],
        compiler_params=pltpu.CompilerParams(
            collective_id=0, has_side_effects=True, vmem_limit_bytes=63 * 2**20
        ),
    )(
        inputs.reshape(T, D), segment_ids, cotangent.reshape(T, D), qkv_weight, row(query_bias),
        row(value_bias), out_weight, row(out_bias), row(attn_gain), row(attn_shift), up_weight,
        row(up_bias), down_weight, row(down_bias), row(ffn_gain), row(ffn_shift),
    )
    r = pl.pallas_call(
        finish,
        out_shape=whole + tuple(jax.ShapeDtypeStruct((1, n), F32) for _, n in VECTORS),
        in_specs=[hbm] * 6 + [vmem],
        out_specs=(hbm,) * 6 + (vmem,) * 9,
        scratch_shapes=[pltpu.VMEM(a.shape, a.dtype) for a in whole] + [pltpu.SemaphoreType.DMA((2, 6))],
    )(*outs)
    v = [a.reshape(-1) for a in r[6:]]
    return (
        r[0].reshape(1, T, D), r[1].reshape(1, T, D), r[2], v[0], v[1], r[3], v[2], v[3], v[4], r[4], v[5],
        r[5], v[6], v[7], v[8],
    )


def solution(mesh):
    pages = P(("dp", "fsdp"), None, None)
    mat = P("fsdp", None)
    v = P("fsdp")
    in_specs = (pages, P(("dp", "fsdp"), None), pages, mat, v, v, mat, v, v, v, mat, v, mat, v, v, v)
    out_specs = (pages, pages, mat, v, v, mat, v, v, v, mat, v, mat, v, v, v)
    return jax.shard_map(body, mesh=mesh, in_specs=in_specs, out_specs=out_specs, check_vma=False)
```
